32 devices in a mesh: dp: 8 (over z, core), space: 4 (over y, x).
Axes of the slice: x: 2, y: 2, z: 4, core: 2. Of those that a mesh axis runs over, the one named last changes fastest.
Arguments:
- features: bfloat16 [8, 40, 37, 1024], P('dp', 'space'), may hold values from -6 to 6
- weights: bfloat16 [3, 9, 1024, 128], P(None, None, 'space'), may hold values from -0.0625 to 0.0625
- bias: float32 [3, 128], replicated, may hold values from -3 to 3
- grad_out: bfloat16 [8, 40, 37, 384], P('dp', 'space'), may hold values from -6 to 6
Outputs:
- activations: bfloat16 [8, 40, 37, 384], P('dp', 'space')
- input_grad: bfloat16 [8, 40, 37, 1024], P('dp', 'space')
- weight_grad: float32 [3, 9, 1024, 128], P(None, None, 'space')
- bias_grad: float32 [3, 128], replicated
The draws below stay inside these ranges and needn't reach their ends.
All inputs are finite; a program needn't handle non-finite values.
Results may differ from the reference program's by a relative error of at most 0.0049.
Values may be sent and summed in bfloat16 or wider, within the bound.
No kernel may reach another device: no remote copies, remote signals or barrier semaphores. Data moves between devices by JAX's collectives and lax.ppermute only.
A program may use at most 128 MiB of HBM per device.

```python
import jax
import jax.numpy as jnp
from jax import lax

CIN = 1024
COUT = 128
H = 40
W = 37
B = 8


def levels(rng, dims, cuts, low, largest):
    loudness, own = 1.0, jax.random.fold_in(rng, 6)
    for axis_at, shards_of in cuts:
        steps = jnp.exp(jax.random.uniform(jax.random.fold_in(own, axis_at), (shards_of,), jnp.float32, low / len(cuts), largest / len(cuts)))
        loudness = loudness * jnp.repeat(steps, dims[axis_at] // shards_of).reshape([-1 if axis == axis_at else 1 for axis in range(len(dims))])
    return loudness


def centred(own_key, shape, deviation, reach, split=(), kind=jnp.bfloat16):
    loudness = levels(own_key, shape, split, -0.22, 0.18) if split else 1.0
    result = jax.random.normal(own_key, shape, jnp.float32) * deviation * loudness
    return jnp.minimum(jnp.maximum(result, -reach), reach).astype(kind)


def setup_inputs(seed: int = 0) -> dict:
    arg_keys = jax.random.split(jax.random.key(seed), 5)
    features = centred(arg_keys[0], (B, H, W, CIN), 1.0, 6.0, ((0, 8), (1, 4)))
    weights = centred(arg_keys[1], (3, 9, CIN, COUT), (9 * CIN) ** -0.5, 0.0625, ((2, 4),))
    bias = centred(arg_keys[2], (3, COUT), 0.5, 3.0, (), jnp.float32)
    grad_out = centred(arg_keys[3], (B, H, W, 3 * COUT), 1.0, 6.0, ((0, 8), (1, 4)))
    return dict(features=features, weights=weights, bias=bias, grad_out=grad_out)


dilations = (12, 24, 36)
offsets = tuple((row_shift, col_shift) for row_shift in (-1, 0, 1) for col_shift in (-1, 0, 1))


def valid_span(shift, length):
    return max(0, -shift), length - max(0, shift)


def reference(features, weights, bias, grad_out):
    image_count, height, columns, channels = features.shape
    outputs = weights.shape[3]
    pixels = height * columns

    def one_image(totals, inputs_now):
        picture, upstream = inputs_now
        pre_parts = []
        for branch, spacing in enumerate(dilations):
            running = jnp.zeros((height, columns, outputs), jnp.float32)
            for tap_index, (shift_y, shift_x) in enumerate(offsets):
                step_y = shift_y * spacing
                step_x = shift_x * spacing
                row_lo, row_hi = valid_span(step_y, height)
                col_lo, col_hi = valid_span(step_x, columns)
                window = picture[row_lo + step_y:row_hi + step_y, col_lo + step_x:col_hi + step_x, :]
                product = jnp.dot(window.reshape(-1, channels), weights[branch, tap_index], preferred_element_type=jnp.float32)
                running = running.at[row_lo:row_hi, col_lo:col_hi, :].add(product.reshape(row_hi - row_lo, col_hi - col_lo, outputs))
            pre_parts.append(running.reshape(pixels, outputs) + bias[branch])
        pre_act = jnp.concatenate(pre_parts, axis=1)
        squash = jax.nn.sigmoid(pre_act)
        active = (pre_act * squash).astype(jnp.bfloat16)
        slope_terms = squash * (1.0 + pre_act * (1.0 - squash))
        grad_pre = (upstream.reshape(pixels, 3 * outputs).astype(jnp.float32) * slope_terms).astype(jnp.bfloat16)
        grad_map = grad_pre.reshape(height, columns, 3 * outputs)
        grad_input = jnp.zeros((height, columns, channels), jnp.float32)
        weight_parts = []
        bias_parts = []
        for branch, spacing in enumerate(dilations):
            first_col = branch * outputs
            branch_grad = grad_map[:, :, first_col:first_col + outputs]
            bias_parts.append(jnp.sum(branch_grad.astype(jnp.float32), axis=(0, 1)))
            tap_terms = []
            for tap_index, (shift_y, shift_x) in enumerate(offsets):
                step_y = shift_y * spacing
                step_x = shift_x * spacing
                row_lo, row_hi = valid_span(step_y, height)
                col_lo, col_hi = valid_span(step_x, columns)
                window = picture[row_lo + step_y:row_hi + step_y, col_lo + step_x:col_hi + step_x, :].reshape(-1, channels)
                grad_piece = branch_grad[row_lo:row_hi, col_lo:col_hi, :].reshape(-1, outputs)
                tap_terms.append(jnp.dot(window.T, grad_piece, preferred_element_type=jnp.float32))
                back = jnp.dot(grad_piece, weights[branch, tap_index].T, preferred_element_type=jnp.float32)
                grad_input = grad_input.at[row_lo + step_y:row_hi + step_y, col_lo + step_x:col_hi + step_x, :].add(back.reshape(row_hi - row_lo, col_hi - col_lo, channels))
            weight_parts.append(jnp.stack(tap_terms))
        totals = (totals[0] + jnp.stack(weight_parts), totals[1] + jnp.stack(bias_parts))
        return totals, (active.reshape(height, columns, 3 * outputs), grad_input.astype(jnp.bfloat16))

    initial = (jnp.zeros((3, 9, channels, outputs), jnp.float32), jnp.zeros((3, outputs), jnp.float32))
    (weight_sum, bias_sum), (activations, input_grad) = lax.scan(one_image, initial, (features, grad_out))
    return activations, input_grad, weight_sum / image_count, bias_sum / image_count
```

```python
import functools

import jax
import jax.numpy as jnp
from jax import lax
from jax.experimental import pallas as pl
from jax.experimental.pallas import tpu as pltpu
from jax.sharding import PartitionSpec as P

dilations = (12, 24, 36)
BF = jnp.bfloat16
F32 = jnp.float32
EXTRA = 16


def stride_of(columns):
    return -(-columns // 8) * 8


def call(kernel, ins, outs, scratch, name, flops=0, in_specs=None):
    nbytes = sum(x.size * x.dtype.itemsize for x in ins) + sum(
        x.size * x.dtype.itemsize for x in outs
    )
    vmem = pl.BlockSpec(memory_space=pltpu.VMEM)
    return pl.pallas_call(
        kernel,
        grid=(1,),
        out_shape=tuple(outs),
        in_specs=in_specs or [vmem] * len(ins),
        out_specs=tuple(vmem for _ in outs),
        scratch_shapes=scratch,
        name=name,
        compiler_params=pltpu.CompilerParams(vmem_limit_bytes=48 * 1024 * 1024),
        cost_estimate=pl.CostEstimate(flops=flops, bytes_accessed=nbytes, transcendentals=0),
    )(*ins)


def shape(dims, kind):
    return jax.ShapeDtypeStruct(dims, kind)


def flatten_rows(src, scr, rows, columns, stride):
    for r in range(rows):
        scr[stride * r : stride * r + columns] = src[0, r].astype(F32)
        if stride > columns:
            scr[stride * r + columns : stride * (r + 1)] = jnp.zeros(
                (stride - columns, scr.shape[1]), F32
            )


def split_kernel(dims, x_ref, *refs):
    rows, columns, stride, parts = dims
    outs, scr = refs[:parts], refs[parts]
    me = lax.axis_index("space")
    flatten_rows(x_ref, scr, rows, columns, stride)
    width = outs[0].shape[1]
    for b in range(parts):
        at = pl.multiple_of((me ^ b) * width, width)
        outs[b][...] = scr[:, pl.ds(at, width)].astype(BF)


def shifted_copies(pad_scr, half_scr, out, columns, stride, shifts):
    total, n = out.shape[0], pad_scr.shape[1]
    pad = (pad_scr.shape[0] - total) // 2
    limit = pad_scr.shape[0] - 8
    half_scr[0:limit] = pad_scr[4 : limit + 4]
    step = 2 * stride
    col = lax.broadcasted_iota(jnp.int32, (step, n), 0)
    col = jnp.where(col >= stride, col - stride, col)

    @pl.loop(0, total // step)
    def _(p):
        base = pl.multiple_of(p * step, step)
        for j, shift in enumerate(shifts):
            off = pad + shift
            if off % 8 == 0:
                v = pad_scr[pl.ds(pl.multiple_of(base + off, 8), step)]
            else:
                v = half_scr[pl.ds(pl.multiple_of(base + off - 4, 8), step)]
            if shift:
                ok = (col + shift >= 0) & (col + shift < columns)
                v = jnp.where(ok, v, 0.0)
            out[pl.ds(base, step), j * n : (j + 1) * n] = v.astype(BF)


def gather_blocks(blocks, pad_scr, pad):
    me = lax.axis_index("space")
    size, n = blocks[0].shape
    total = size * len(blocks)
    pad_scr[0:pad] = jnp.zeros((pad, n), F32)
    pad_scr[pad + total : 2 * pad + total] = jnp.zeros((pad, n), F32)
    for b, block in enumerate(blocks):
        at = pl.multiple_of((me ^ b) * size + pad, 8)
        pad_scr[pl.ds(at, size)] = block[...].astype(F32)


def mm(a, b, ca=1, cb=0):
    return lax.dot_general(a, b, (((ca,), (cb,)), ((), ())), preferred_element_type=F32)


def forward_kernel(dims, spacing, parts, w_ref, *refs):
    columns, stride = dims
    blocks, outs = refs[:parts], refs[parts : 2 * parts]
    pad_scr, half_scr, stack, acc = refs[2 * parts :]
    me = lax.axis_index("space")
    total = acc.shape[0]
    n = blocks[0].shape[1]
    gather_blocks(blocks, pad_scr, stride)
    shifted_copies(pad_scr, half_scr, stack, columns, stride, (-spacing, 0, spacing))
    step = spacing * stride
    taps = [w_ref[0, 3 * a : 3 * a + 3].reshape(3 * n, w_ref.shape[3]) for a in range(3)]
    acc[...] = mm(stack[...], taps[1])
    acc[step:] += mm(stack[: total - step], taps[0])
    acc[: total - step] += mm(stack[step:], taps[2])
    size = outs[0].shape[0]
    for b in range(parts):
        at = pl.multiple_of((me ^ b) * size, 8)
        outs[b][...] = acc[pl.ds(at, size)].astype(outs[b].dtype)


def act_kernel(dims, branch, parts, *refs):
    rows, columns, stride = dims
    partials, bias_ref, go_ref = refs[:parts], refs[parts], refs[parts + 1]
    act_ref, grad_ref, scr = refs[parts + 2 :]
    flatten_rows(go_ref, scr, rows, columns, stride)
    pre = partials[0][...]
    for part in partials[1:]:
        pre = pre + part[...].astype(F32)
    pre = pre + bias_ref[branch : branch + 1, :]
    squash = jax.nn.sigmoid(pre)
    slope = squash * (1.0 + pre * (1.0 - squash))
    grad_ref[...] = (scr[...] * slope).astype(BF)
    scr[...] = pre * squash
    for r in range(rows):
        act_ref[0, r] = scr[stride * r : stride * r + columns].astype(BF)


def weight_kernel(dims, spacing, parts, *refs):
    columns, stride = dims
    grads, feats = refs[:parts], refs[parts : 2 * parts]
    keep, send = refs[2 * parts : 2 * parts + 2]
    gpad, ghalf, gstack, fpad, feat, full = refs[2 * parts + 2 :]
    core = lax.axis_index("dp") % 2
    total = gstack.shape[0]
    outputs = gpad.shape[1]
    gather_blocks(grads, gpad, stride)
    shifted_copies(gpad, ghalf, gstack, columns, stride, (spacing, 0, -spacing))
    me = lax.axis_index("space")
    size = feats[0].shape[0]
    for b in range(parts):
        at = pl.multiple_of((me ^ b) * size, 8)
        fpad[pl.ds(at, size)] = feats[b][...].astype(F32)
    feat[...] = fpad[...].astype(BF)
    step = spacing * stride
    for a in range(3):
        if a == 0:
            f, g = feat[: total - step], gstack[step:]
        elif a == 1:
            f, g = feat[...], gstack[...]
        else:
            f, g = feat[step:], gstack[: total - step]
        r = mm(f, g, 0, 0)
        for c in range(3):
            full[3 * a + c] = r[:, c * outputs : (c + 1) * outputs]
    half = full.shape[1] // 2
    body = 9 * half
    mine = full[:, pl.ds(pl.multiple_of(core * half, half), half)]
    other = full[:, pl.ds(pl.multiple_of((1 - core) * half, half), half)]
    keep[:body] = mine.reshape(body, outputs)
    send[:body] = other.reshape(body, outputs).astype(BF)
    total_bias = jnp.sum(gpad[...], axis=0, keepdims=True)
    high = total_bias.astype(BF).astype(F32)
    low = total_bias - high
    row = lax.broadcasted_iota(jnp.int32, (EXTRA, outputs), 0)
    keep[body:] = jnp.where(row == 0, total_bias, 0.0)
    send[body:] = jnp.where(row == 0, high, jnp.where(row == 1, low, 0.0)).astype(BF)


def fold_extra(x):
    row = lax.broadcasted_iota(jnp.int32, x.shape, 0)
    return jnp.where(row == 0, jnp.sum(x, axis=0, keepdims=True), 0.0)


def pack_extra(x):
    total = jnp.sum(x, axis=0, keepdims=True)
    high = total.astype(BF).astype(F32)
    row = lax.broadcasted_iota(jnp.int32, x.shape, 0)
    return jnp.where(row == 0, high, jnp.where(row == 1, total - high, 0.0)).astype(BF)


def add_pack_kernel(a_ref, b_ref, out_ref):
    body = out_ref.shape[0] - EXTRA
    total = a_ref[...].astype(F32) + b_ref[...].astype(F32)
    out_ref[:body] = total[:body].astype(BF)
    out_ref[body:] = pack_extra(total[body:])


def round_kernel(a_ref, out_ref):
    body = out_ref.shape[0] - EXTRA
    out_ref[:body] = a_ref[:body].astype(BF)
    out_ref[body:] = pack_extra(a_ref[body:])


def weight_out_kernel(scale, n, *refs):
    ins, (w_ref, b_ref) = refs[: 2 * n], refs[2 * n :]
    core = lax.axis_index("dp") % 2
    for k in range(n):
        mine, other = ins[2 * k], ins[2 * k + 1]
        half = w_ref.shape[2] // 2
        outputs = w_ref.shape[3]
        body = 9 * half
        at = pl.multiple_of(core * half, half)
        w_ref[k, :, pl.ds(at, half)] = (mine[:body].astype(F32) * scale).reshape(9, half, outputs)
        at = pl.multiple_of((1 - core) * half, half)
        w_ref[k, :, pl.ds(at, half)] = (other[:body].astype(F32) * scale).reshape(9, half, outputs)
        extra = jnp.sum(mine[body:].astype(F32), axis=0, keepdims=True)
        b_ref[k : k + 1, :] = extra * scale


def input_kernel(dims, parts, w_ref, *refs):
    columns, stride = dims
    grads, outs = refs[: 3 * parts], refs[3 * parts : 4 * parts]
    gpad, ghalf, gstack, acc = refs[4 * parts :]
    me = lax.axis_index("space")
    total = acc.shape[0]
    outputs = w_ref.shape[3]
    for k, spacing in enumerate(dilations):
        gather_blocks(grads[k * parts : (k + 1) * parts], gpad, stride)
        shifted_copies(gpad, ghalf, gstack, columns, stride, (spacing, 0, -spacing))
        step = spacing * stride
        for a in (1, 0, 2):
            w = jnp.concatenate([w_ref[k, 3 * a + c] for c in range(3)], axis=1)
            if a == 1:
                r = mm(gstack[...], w, 1, 1)
                if k == 0:
                    acc[...] = r
                else:
                    acc[...] += r
            elif a == 0:
                acc[: total - step] += mm(gstack[step:], w, 1, 1)
            else:
                acc[step:] += mm(gstack[: total - step], w, 1, 1)
    size = outs[0].shape[0]
    for b in range(parts):
        at = pl.multiple_of((me ^ b) * size, 8)
        outs[b][...] = acc[pl.ds(at, size)].astype(BF)


def join_kernel(dims, parts, *refs):
    rows, columns, stride = dims
    blocks, out_ref, scr = refs[:parts], refs[parts], refs[parts + 1]
    me = lax.axis_index("space")
    width = blocks[0].shape[1]
    for b in range(parts):
        at = pl.multiple_of((me ^ b) * width, width)
        scr[:, pl.ds(at, width)] = blocks[b][...].astype(F32)
    for r in range(rows):
        out_ref[0, r] = scr[stride * r : stride * r + columns].astype(BF)


def merge_kernel(*refs):
    ins, out = refs[:-1], refs[-1]
    n = ins[0].shape[3]
    for k, x in enumerate(ins):
        out[:, :, :, k * n : (k + 1) * n] = x[...]


def swap(x, bit):
    n = lax.axis_size("space")
    return lax.ppermute(x, "space", [(i, i ^ bit) for i in range(n)])


def line_sum(kept, size):
    rows, outputs = kept.shape
    n = size // 2
    packed = shape((rows, outputs), BF)
    if n != 4:
        groups = [[2 * i + c for i in range(n)] for c in range(2)]
        total = lax.psum(kept, "dp", axis_index_groups=groups)
        return call(round_kernel, [total], [packed], [], "round_rows")[0]
    start = call(round_kernel, [kept], [packed], [], "round_rows")[0]

    def chips(pairs):
        return [(2 * a + c, 2 * b + c) for a, b in pairs for c in range(2)]

    inward = lax.ppermute(start, "dp", chips([(0, 1), (3, 2)]))
    near = call(add_pack_kernel, [kept, inward], [packed], [], "add_near")[0]
    across = lax.ppermute(near, "dp", chips([(1, 2), (2, 1)]))
    total = call(add_pack_kernel, [near, across], [packed], [], "add_far")[0]
    outward = lax.ppermute(total, "dp", chips([(1, 0), (2, 3)]))
    chip = lax.axis_index("dp") // 2
    inner = (chip == 1) | (chip == 2)
    return jnp.where(inner, total, outward)


def per_device(features, weights, bias, grad_out):
    images, rows, columns, channels_all = features.shape
    assert images == 1
    parts = lax.axis_size("space")
    dp = lax.axis_size("dp")
    channels, outputs = weights.shape[2], weights.shape[3]
    stride = stride_of(columns)
    size = rows * stride
    total = size * parts
    padded = total + 2 * stride
    vm = pltpu.VMEM

    mine = call(
        functools.partial(split_kernel, (rows, columns, stride, parts)),
        [features],
        [shape((size, channels), BF)] * parts,
        [vm((size, channels_all), F32)],
        "split_channels",
    )
    feats = [mine[0]] + [swap(mine[b], b) for b in range(1, parts)]

    def branch_weights(k):
        return pl.BlockSpec((1, 9, channels, outputs), lambda i: (k, 0, 0, 0))

    whole = pl.BlockSpec(memory_space=pltpu.VMEM)
    acts, grads, sums = [], [], []
    partials = []
    for k, spacing in enumerate(dilations):
        part = call(
            functools.partial(forward_kernel, (columns, stride), spacing, parts),
            [weights] + feats,
            [shape((size, outputs), F32)] + [shape((size, outputs), BF)] * (parts - 1),
            [
                vm((padded, channels), F32),
                vm((padded, channels), F32),
                vm((total, 3 * channels), BF),
                vm((total, outputs), F32),
            ],
            f"forward_{k}",
            flops=2 * total * 6 * channels * outputs,
            in_specs=[branch_weights(k)] + [whole] * parts,
        )
        partials.append([part[0]] + [swap(part[b], b) for b in range(1, parts)])
    for k in range(3):
        act, grad = call(
            functools.partial(act_kernel, (rows, columns, stride), k, parts),
            partials[k] + [bias, grad_out],
            [shape((1, rows, columns, outputs), BF), shape((size, outputs), BF)],
            [vm((size, outputs), F32)],
            f"activation_{k}",
            in_specs=[whole] * (parts + 1)
            + [pl.BlockSpec((1, rows, columns, outputs), lambda i, k=k: (0, 0, 0, k))],
        )
        acts.append(act)
        grads.append([grad] + [swap(grad, b) for b in range(1, parts)])
    half = channels // 2
    kept_rows = 9 * half + EXTRA
    for k, spacing in enumerate(dilations):
        keep, send = call(
            functools.partial(weight_kernel, (columns, stride), spacing, parts),
            grads[k] + feats,
            [shape((kept_rows, outputs), F32), shape((kept_rows, outputs), BF)],
            [
                vm((padded, outputs), F32),
                vm((padded, outputs), F32),
                vm((total, 3 * outputs), BF),
                vm((total, channels), F32),
                vm((total, channels), BF),
                vm((9, channels, outputs), F32),
            ],
            f"weight_grad_{k}",
            flops=2 * total * 6 * channels * outputs,
        )
        other = lax.ppermute(send, "dp", [(i, i ^ 1) for i in range(dp)])
        kept = call(
            add_fold_kernel,
            [keep, other],
            [shape((kept_rows, outputs), F32)],
            [],
            "add_cores",
        )[0]
        sums.append(line_sum(kept, dp))
    back = call(
        functools.partial(input_kernel, (columns, stride), parts),
        [weights] + grads[0] + grads[1] + grads[2],
        [shape((size, channels), BF)] * parts,
        [
            vm((padded, outputs), F32),
            vm((padded, outputs), F32),
            vm((total, 3 * outputs), BF),
            vm((total, channels), F32),
        ],
        "input_grad",
        flops=2 * total * 18 * channels * outputs,
    )
    blocks = [back[0]] + [swap(back[b], b) for b in range(1, parts)]
    input_grad = call(
        functools.partial(join_kernel, (rows, columns, stride), parts),
        blocks,
        [shape(features.shape, BF)],
        [vm((size, channels_all), F32)],
        "join_channels",
    )[0]
    active = call(merge_kernel, acts, [shape(grad_out.shape, BF)], [], "merge_branches")[0]
    final = []
    for s in sums:
        final += [s, lax.ppermute(s, "dp", [(i, i ^ 1) for i in range(dp)])]
    weight_grad, bias_grad = call(
        functools.partial(weight_out_kernel, 1.0 / dp, 3),
        final,
        [shape((3, 9, channels, outputs), F32), shape((3, outputs), F32)],
        [],
        "weight_grad_out",
    )
    return active, input_grad, weight_grad, bias_grad


def add_fold_kernel(a_ref, b_ref, out_ref):
    body = out_ref.shape[0] - EXTRA
    total = a_ref[...] + b_ref[...].astype(F32)
    out_ref[:body] = total[:body]
    out_ref[body:] = fold_extra(total[body:])


def solution(mesh):
    placed = (
        P("dp", "space", None, None),
        P(None, None, "space", None),
        P(),
        P("dp", "space", None, None),
    )
    return jax.shard_map(
        per_device,
        mesh=mesh,
        in_specs=placed,
        out_specs=(
            P("dp", "space", None, None),
            P("dp", "space", None, None),
            P(None, None, "space", None),
            P(),
        ),
        check_vma=False,
    )
```

```python
import functools

import jax
import jax.numpy as jnp
from jax import lax
from jax.experimental import pallas as pl
from jax.experimental.pallas import tpu as pltpu
from jax.sharding import PartitionSpec as P

dilations = (12, 24, 36)
BF = jnp.bfloat16
F32 = jnp.float32
EXTRA = 16


def stride_of(columns):
    return -(-columns // 8) * 8


COSTS = {"input_grad": 0.05, "add_near_0": 0.05, "add_near_1": 0.05, "add_near_2": 0.05, "split_rows": 0.05, "add_far_0": 0.05, "add_far_1": 0.05, "add_far_2": 0.05, "merge_branches": 0.05, "join_channels": 0.05, "choose_0": 0.05, "choose_1": 0.05, "choose_2": 0.05, "weight_out_0": 0.05, "weight_out_1": 0.05, "weight_out_2": 0.05, "bias_out": 0.05}
UNIT = 1_150_000_000


def call(chain, kernel, ins, outs, scratch, name, in_specs=None, out_specs=None, aliases=None):
    after = chain[-1:]
    vmem = pl.BlockSpec(memory_space=pltpu.VMEM)
    specs = list(in_specs or [vmem] * len(ins)) + [pl.BlockSpec(memory_space=pl.ANY)] * len(after)
    n, m, k = len(ins), len(after), len(outs)

    def body(*refs):
        token = refs[n + m + k]
        token[...] = jnp.zeros(token.shape, F32)
        kernel(*refs[:n], *refs[n + m : n + m + k], *refs[n + m + k + 1 :])

    *got, token = pl.pallas_call(
        body,
        grid=(1,),
        out_shape=(*outs, shape((8, 128), F32)),
        in_specs=specs,
        out_specs=(*(out_specs or [vmem] * k), vmem),
        scratch_shapes=scratch,
        name=name,
        input_output_aliases=aliases or {},
        compiler_params=pltpu.CompilerParams(vmem_limit_bytes=40 * 1024 * 1024),
        cost_estimate=pl.CostEstimate(
            flops=int(COSTS.get(name, 1.0) * UNIT), bytes_accessed=1024, transcendentals=0
        ),
    )(*ins, *after)
    chain.append(token)
    return got


def shape(dims, kind):
    return jax.ShapeDtypeStruct(dims, kind)


def flatten_rows(src, scr, rows, columns, stride):
    for r in range(rows):
        scr[stride * r : stride * r + columns] = src[0, r].astype(F32)
        if stride > columns:
            scr[stride * r + columns : stride * (r + 1)] = jnp.zeros(
                (stride - columns, scr.shape[1]), F32
            )


def levels(parts):
    return parts.bit_length() - 1


def flip_bit(core, level, parts):
    return 1 << ((level + core) % levels(parts))


def owner(q, parts):
    core = lax.axis_index("dp") % 2
    at = lax.axis_index("space")
    for level in range(levels(parts)):
        if (q >> (levels(parts) - 1 - level)) & 1:
            at = at ^ jnp.where(core == 0, flip_bit(0, level, parts), flip_bit(1, level, parts))
    return at


def exchange(x, level, parts, dp):
    pairs = []
    for d in range(dp):
        for p in range(parts):
            pairs.append((d * parts + p, d * parts + (p ^ flip_bit(d % 2, level, parts))))
    return lax.ppermute(x, ("dp", "space"), pairs)


def split_kernel(dims, x_ref, *refs):
    rows, columns, stride, parts = dims
    outs, scr = refs[:parts], refs[parts]
    me = lax.axis_index("space")
    flatten_rows(x_ref, scr, rows, columns, stride)
    width = outs[0].shape[1]
    for b in range(parts):
        at = pl.multiple_of((me ^ b) * width, width)
        outs[b][...] = scr[:, pl.ds(at, width)].astype(BF)


def shifted_copies(pad_scr, half_scr, out, columns, stride, shifts):
    total, n = out.shape[0], pad_scr.shape[1]
    pad = (pad_scr.shape[0] - total) // 2
    limit = pad_scr.shape[0] - 8
    half_scr[0:limit] = pad_scr[4 : limit + 4]
    step = 2 * stride
    col = lax.broadcasted_iota(jnp.int32, (step, n), 0)
    col = jnp.where(col >= stride, col - stride, col)

    @pl.loop(0, total // step)
    def _(p):
        base = pl.multiple_of(p * step, step)
        for j, shift in enumerate(shifts):
            off = pad + shift
            if off % 8 == 0:
                v = pad_scr[pl.ds(pl.multiple_of(base + off, 8), step)]
            else:
                v = half_scr[pl.ds(pl.multiple_of(base + off - 4, 8), step)]
            if shift:
                ok = (col + shift >= 0) & (col + shift < columns)
                v = jnp.where(ok, v, 0.0)
            out[pl.ds(base, step), j * n : (j + 1) * n] = v.astype(BF)


def gather_blocks(blocks, pad_scr, pad):
    me = lax.axis_index("space")
    size, n = blocks[0].shape
    total = size * len(blocks)
    pad_scr[0:pad] = jnp.zeros((pad, n), F32)
    pad_scr[pad + total : 2 * pad + total] = jnp.zeros((pad, n), F32)
    for b, block in enumerate(blocks):
        at = pl.multiple_of((me ^ b) * size + pad, 8)
        pad_scr[pl.ds(at, size)] = block[...].astype(F32)


def mm(a, b, ca=1, cb=0):
    return lax.dot_general(a, b, (((ca,), (cb,)), ((), ())), preferred_element_type=F32)


def take_rows(scr, places, size, parts):
    rows = [scr[pl.ds(pl.multiple_of(owner(q, parts) * size, 8), size)] for q in places]
    return jnp.concatenate(rows, axis=0)


def forward_kernel(dims, branch, parts, w_ref, *refs):
    columns, stride = dims
    blocks, outs = refs[:parts], refs[parts:-6]
    pad_scr, half_scr, stack, acc, taps, sem = refs[-6:]
    copy = pltpu.make_async_copy(w_ref.at[branch], taps, sem)
    copy.start()
    spacing = dilations[branch]
    total = acc.shape[0]
    n = blocks[0].shape[1]
    gather_blocks(blocks, pad_scr, stride)
    shifted_copies(pad_scr, half_scr, stack, columns, stride, (-spacing, 0, spacing))
    copy.wait()
    step = spacing * stride
    w = [taps[3 * a : 3 * a + 3].reshape(3 * n, taps.shape[2]) for a in range(3)]
    acc[...] = mm(stack[...], w[1])
    acc[step:] += mm(stack[: total - step], w[0])
    acc[: total - step] += mm(stack[step:], w[2])
    keep, send = outs[:2]
    size = blocks[0].shape[0]
    keep[...] = take_rows(acc, range(parts // 2), size, parts)
    send[...] = take_rows(acc, range(parts // 2, parts), size, parts).astype(BF)
    if len(outs) > 2:
        outs[2][...] = stack[:, n : 2 * n]


def add_half_kernel(kept, got, keep, send):
    x = kept[...] + got[...].astype(F32)
    size = keep.shape[0]
    keep[...] = x[:size]
    send[...] = x[size:].astype(BF)


def join_rows_kernel(a, b, out):
    out[...] = jnp.concatenate([a[...].astype(F32), b[...].astype(F32)], axis=0).astype(BF)


def act_kernel(dims, branch, kept, got, bias_ref, go_ref, act_ref, grad_ref, scr):
    rows, columns, stride = dims
    flatten_rows(go_ref, scr, rows, columns, stride)
    pre = kept[...] + got[...].astype(F32) + bias_ref[branch : branch + 1, :]
    squash = jax.nn.sigmoid(pre)
    slope = squash * (1.0 + pre * (1.0 - squash))
    grad_ref[...] = (scr[...] * slope).astype(BF)
    scr[...] = pre * squash
    for r in range(rows):
        act_ref[0, r] = scr[stride * r : stride * r + columns].astype(BF)


def weight_kernel(dims, spacing, parts, mine, theirs, feat, keep, send, gstack, *scratch):
    columns, stride = dims
    gpad, ghalf, full = scratch
    core = lax.axis_index("dp") % 2
    total = gstack.shape[0]
    outputs = gpad.shape[1]
    size = total // parts
    gpad[0:stride] = jnp.zeros((stride, outputs), F32)
    gpad[stride + total :] = jnp.zeros((stride, outputs), F32)
    for q in range(parts):
        block = (mine, theirs)[2 * q // parts][...].astype(F32)
        at = q % (parts // 2) * size
        to = pl.multiple_of(owner(q, parts) * size + stride, 8)
        gpad[pl.ds(to, size)] = block[at : at + size]
    shifted_copies(gpad, ghalf, gstack, columns, stride, (spacing, 0, -spacing))
    step = spacing * stride
    for a in range(3):
        if a == 0:
            f, g = feat[: total - step], gstack[step:]
        elif a == 1:
            f, g = feat[...], gstack[...]
        else:
            f, g = feat[step:], gstack[: total - step]
        r = mm(f, g, 0, 0)
        for c in range(3):
            full[3 * a + c] = r[:, c * outputs : (c + 1) * outputs]
    half = full.shape[1] // 2
    body = 9 * half
    own = full[:, pl.ds(pl.multiple_of(core * half, half), half)]
    other = full[:, pl.ds(pl.multiple_of((1 - core) * half, half), half)]
    keep[:body] = own.reshape(body, outputs)
    send[:body] = other.reshape(body, outputs).astype(BF)
    total_bias = jnp.sum(gpad[...], axis=0, keepdims=True)
    row = lax.broadcasted_iota(jnp.int32, (EXTRA, outputs), 0)
    own_bias = jnp.where(row == 0, total_bias, 0.0)
    keep[body:] = own_bias
    send[body:] = pack_extra(own_bias)


def pack_extra(x):
    total = jnp.sum(x, axis=0, keepdims=True)
    high = total.astype(BF).astype(F32)
    row = lax.broadcasted_iota(jnp.int32, x.shape, 0)
    return jnp.where(row == 0, high, jnp.where(row == 1, total - high, 0.0)).astype(BF)


def add_pack_kernel(*refs):
    ins, out_ref = refs[:-1], refs[-1]
    body = out_ref.shape[0] - EXTRA
    total = ins[0][...].astype(F32)
    for x in ins[1:]:
        total = total + x[...].astype(F32)
    out_ref[:body] = total[:body].astype(BF)
    out_ref[body:] = pack_extra(total[body:])


def choose_kernel(inner_ref, outer_ref, out_ref):
    chip = lax.axis_index("dp") // 2
    inner = (chip == 1) | (chip == 2)
    out_ref[...] = jnp.where(inner, inner_ref[...], outer_ref[...])


def weight_out_kernel(scale, place, first, *refs):
    mine, other = refs[:2]
    out, full, sem = refs[2 if first else 3 :]
    core = lax.axis_index("dp") % 2
    half, outputs = full.shape[1] // 2, full.shape[2]
    body = 9 * half
    for x, at in ((mine, core), (other, 1 - core)):
        rows = (x[:body].astype(F32) * scale).reshape(9, half, outputs)
        full[:, pl.ds(pl.multiple_of(at * half, half), half)] = rows
    copy = pltpu.make_async_copy(full, out.at[place], sem)
    copy.start()
    copy.wait()


def bias_out_kernel(scale, *refs):
    ins, out = refs[:-1], refs[-1]
    for k, x in enumerate(ins):
        extra = x[x.shape[0] - EXTRA :].astype(F32)
        out[k : k + 1, :] = jnp.sum(extra, axis=0, keepdims=True) * scale


def touch_kernel(w_ref):
    pass


def input_kernel(dims, parts, w_ref, *refs):
    stacks = refs[:3]
    acc, taps, sem = refs[3:]
    copy = pltpu.make_async_copy(w_ref, taps, sem)
    copy.start()
    copy.wait()
    total = acc.shape[0]
    for k, spacing in enumerate(dilations):
        g = stacks[k]
        step = spacing * dims[1]
        for a in (1, 0, 2):
            w = jnp.concatenate([taps[k, 3 * a + c] for c in range(3)], axis=1)
            if a == 1:
                r = mm(g[...], w, 1, 1)
                if k == 0:
                    acc[...] = r
                else:
                    acc[...] += r
            elif a == 0:
                acc[: total - step] += mm(g[step:], w, 1, 1)
            else:
                acc[step:] += mm(g[: total - step], w, 1, 1)


def split_rows_kernel(parts, acc, *outs):
    me = lax.axis_index("space")
    size = outs[0].shape[0]
    for b in range(parts):
        at = pl.multiple_of((me ^ b) * size, 8)
        outs[b][...] = acc[pl.ds(at, size)].astype(BF)


def join_kernel(dims, parts, *refs):
    rows, columns, stride = dims
    blocks, out_ref, scr = refs[:parts], refs[parts], refs[parts + 1]
    me = lax.axis_index("space")
    width = blocks[0].shape[1]
    for b in range(parts):
        at = pl.multiple_of((me ^ b) * width, width)
        scr[:, pl.ds(at, width)] = blocks[b][...].astype(F32)
    for r in range(rows):
        out_ref[0, r] = scr[stride * r : stride * r + columns].astype(BF)


def merge_kernel(*refs):
    ins, out = refs[:-1], refs[-1]
    n = ins[0].shape[3]
    for k, x in enumerate(ins):
        out[:, :, :, k * n : (k + 1) * n] = x[...]


def swap(x, bit):
    n = lax.axis_size("space")
    return lax.ppermute(x, "space", [(i, i ^ bit) for i in range(n)])


def per_device(features, weights, bias, grad_out):
    images, rows, columns, channels_all = features.shape
    assert images == 1
    parts = lax.axis_size("space")
    dp = lax.axis_size("dp")
    channels, outputs = weights.shape[2], weights.shape[3]
    stride = stride_of(columns)
    size = rows * stride
    total = size * parts
    padded = total + 2 * stride
    vm = pltpu.VMEM
    whole = pl.BlockSpec(memory_space=pltpu.VMEM)
    far = pl.BlockSpec(memory_space=pltpu.HBM)
    top = levels(parts)
    cores = [(i, i ^ 1) for i in range(dp)]
    half = channels // 2
    kept_rows = 9 * half + EXTRA
    packed = [shape((kept_rows, outputs), BF)]
    chain = []
    run = functools.partial(call, chain)

    mine = run(
        functools.partial(split_kernel, (rows, columns, stride, parts)),
        [features],
        [shape((size, channels), BF)] * parts,
        [vm((size, channels_all), F32)],
        "split_channels",
    )
    feats = [mine[0]] + [swap(mine[b], b) for b in range(1, parts)]

    state = {}
    rows_kept = size * parts // 2

    def forward(k, with_feat=False):
        outs = [shape((rows_kept, outputs), F32), shape((rows_kept, outputs), BF)]
        if with_feat:
            outs.append(shape((total, channels), BF))
        got = run(
            functools.partial(forward_kernel, (columns, stride), k, parts),
            [weights] + feats,
            outs,
            [
                vm((padded, channels), F32),
                vm((padded, channels), F32),
                vm((total, 3 * channels), BF),
                vm((total, outputs), F32),
                vm((9, channels, outputs), BF),
                pltpu.SemaphoreType.DMA,
            ],
            f"forward_{k}",
            in_specs=[far] + [whole] * parts,
        )
        if with_feat:
            state["feat"] = got[2]
        state[k] = (got[0], exchange(got[1], 0, parts, dp))

    def reduce_step(k, level):
        keep, got = state[k]
        n = keep.shape[0] // 2
        outs = [shape((n, outputs), F32), shape((n, outputs), BF)]
        keep, send = run(add_half_kernel, [keep, got], outs, [], f"add_{k}")
        state[k] = (keep, exchange(send, level, parts, dp))

    def activate(k):
        keep, got = state[k]
        act, grad = run(
            functools.partial(act_kernel, (rows, columns, stride), k),
            [keep, got, bias, grad_out],
            [shape((1, rows, columns, outputs), BF), shape((size, outputs), BF)],
            [vm((size, outputs), F32)],
            f"activation_{k}",
            in_specs=[whole] * 3 + [pl.BlockSpec((1, rows, columns, outputs), lambda i: (0, 0, 0, k))],
        )
        state[k] = (grad, exchange(grad, top - 1, parts, dp))
        state["act", k] = act

    def gather_step(k, level):
        own, got = state[k]
        outs = [shape((2 * own.shape[0], outputs), BF)]
        both = run(join_rows_kernel, [own, got], outs, [], f"join_{k}")[0]
        state[k] = (both, exchange(both, level, parts, dp))

    def weight_part(k):
        own, got = state[k]
        keep, send, stack = run(
            functools.partial(weight_kernel, (columns, stride), dilations[k], parts),
            [own, got, state["feat"]],
            [
                shape((kept_rows, outputs), F32),
                shape((kept_rows, outputs), BF),
                shape((total, 3 * outputs), BF),
            ],
            [
                vm((padded, outputs), F32),
                vm((padded, outputs), F32),
                vm((9, channels, outputs), F32),
            ],
            f"weight_grad_{k}",
        )
        state["stack", k] = stack
        state["sum", k] = (keep, lax.ppermute(send, "dp", cores))

    def line(pairs):
        return [(2 * a + c, 2 * b + c) for a, b in pairs for c in range(2)]

    def add_cores(k):
        keep, other = state["sum", k]
        if dp != 8:
            groups = [[2 * i + c for i in range(dp // 2)] for c in range(2)]
            state["sum", k] = lax.psum(keep + other.astype(F32), "dp", axis_index_groups=groups)
            return
        near = run(add_pack_kernel, [keep, other], packed, [], f"add_cores_{k}")[0]
        state["sum", k] = (keep, other, lax.ppermute(near, "dp", line([(0, 1), (3, 2)])))

    def add_near(k):
        if dp == 8:
            near = run(add_pack_kernel, list(state["sum", k]), packed, [], f"add_near_{k}")[0]
            state["sum", k] = (near, lax.ppermute(near, "dp", line([(1, 2), (2, 1)])))

    def add_far(k):
        if dp != 8:
            state["sum", k] = run(add_pack_kernel, [state["sum", k]], packed, [], f"round_{k}")[0]
            return
        total_rows = run(add_pack_kernel, list(state["sum", k]), packed, [], f"add_far_{k}")[0]
        state["sum", k] = (total_rows, lax.ppermute(total_rows, "dp", line([(1, 0), (2, 3)])))

    def choose(k):
        if dp == 8:
            state["sum", k] = run(choose_kernel, list(state["sum", k]), packed, [], f"choose_{k}")[0]
        state["sum", k] = (state["sum", k], lax.ppermute(state["sum", k], "dp", cores))

    def input_part():
        state["back"] = run(
            functools.partial(input_kernel, (columns, stride), parts),
            [weights] + [state["stack", k] for k in range(3)],
            [shape((total, channels), F32)],
            [vm(weights.shape, BF), pltpu.SemaphoreType.DMA],
            "input_grad",
            in_specs=[far] + [whole] * 3,
        )

    def send_back():
        outs = [shape((size, channels), BF)] * parts
        back = run(functools.partial(split_rows_kernel, parts), state["back"], outs, [], "split_rows")
        state["back"] = [back[0]] + [swap(back[b], b) for b in range(1, parts)]

    def join_back():
        state["input_grad"] = run(
            functools.partial(join_kernel, (rows, columns, stride), parts),
            state["back"],
            [shape(features.shape, BF)],
            [vm((size, channels_all), F32)],
            "join_channels",
        )[0]

    def merge():
        acts = [state["act", k] for k in range(3)]
        state["active"] = run(
            merge_kernel, acts, [shape(grad_out.shape, BF)], [], "merge_branches"
        )[0]

    def weight_out(k):
        first = "weight_grad" not in state
        anywhere = pl.BlockSpec(memory_space=pl.ANY)
        state["weight_grad"] = run(
            functools.partial(weight_out_kernel, 1.0 / dp, k, first),
            list(state["sum", k]) + ([] if first else [state["weight_grad"]]),
            [shape((3, 9, channels, outputs), F32)],
            [vm((9, channels, outputs), F32), pltpu.SemaphoreType.DMA],
            f"weight_out_{k}",
            in_specs=[whole] * 2 + ([] if first else [anywhere]),
            out_specs=[anywhere],
            aliases={} if first else {2: 0},
        )[0]

    k0, k1, k2 = 2, 0, 1
    run(touch_kernel, [weights], [], [], "touch_weights", in_specs=[far])
    forward(k0, with_feat=True)
    forward(k1)
    if top == 2:
        reduce_step(k0, 1)
        forward(k2)
        reduce_step(k1, 1)
        activate(k0)
        reduce_step(k2, 1)
        activate(k1)
        gather_step(k0, 0)
        activate(k2)
        gather_step(k1, 0)
        weight_part(k0)
        gather_step(k2, 0)
        weight_part(k1)
        add_cores(k0)
        weight_part(k2)
        add_cores(k1)
        add_cores(k2)
    else:
        forward(k2)
        for k in (k0, k1, k2):
            for level in range(1, top):
                reduce_step(k, level)
            activate(k)
            for level in range(top - 2, -1, -1):
                gather_step(k, level)
            weight_part(k)
            add_cores(k)
    input_part()
    add_near(k0)
    send_back()
    add_near(k1)
    add_near(k2)
    add_far(k0)
    add_far(k1)
    add_far(k2)
    merge()
    join_back()
    choose(k0)
    choose(k1)
    choose(k2)
    weight_out(k0)
    weight_out(k1)
    weight_out(k2)
    bias_grad = run(
        functools.partial(bias_out_kernel, 1.0 / dp),
        [state["sum", k][0] for k in range(3)],
        [shape((3, outputs), F32)],
        [],
        "bias_out",
    )[0]
    return state["active"], state["input_grad"], state["weight_grad"], bias_grad


def solution(mesh):
    placed = (
        P("dp", "space", None, None),
        P(None, None, "space", None),
        P(),
        P("dp", "space", None, None),
    )
    return jax.shard_map(
        per_device,
        mesh=mesh,
        in_specs=placed,
        out_specs=(
            P("dp", "space", None, None),
            P("dp", "space", None, None),
            P(None, None, "space", None),
            P(),
        ),
        check_vma=False,
    )
```

```python
import functools

import jax
import jax.numpy as jnp
from jax import lax
from jax.experimental import pallas as pl
from jax.experimental.pallas import tpu as pltpu
from jax.sharding import PartitionSpec as P

dilations = (12, 24, 36)
BF = jnp.bfloat16
F32 = jnp.float32
EXTRA = 16


def stride_of(columns):
    return -(-columns // 8) * 8


COSTS = {"input_grad": 0.05, "add_near_0": 0.05, "add_near_1": 0.05, "add_near_2": 0, "split_rows": 0.05, "add_far_0": 0.05, "add_far_1": 0.05, "add_far_2": 0.05, "merge_branches": 0.05, "join_channels": 0.05, "choose_0": 1, "choose_1": 0.05, "choose_2": 0.05, "weight_out_a": 0.05, "weight_out_b": 0.05, "add_cores_2": 1, "join_1": 3, "add_cores_0": 0, "add_cores_1": 0, "weight_grad_1": 0}
UNIT = 1_150_000_000


def call(chain, kernel, ins, outs, scratch, name, in_specs=None, out_specs=None, aliases=None):
    after = chain[-1:]
    vmem = pl.BlockSpec(memory_space=pltpu.VMEM)
    specs = list(in_specs or [vmem] * len(ins)) + [pl.BlockSpec(memory_space=pl.ANY)] * len(after)
    n, m, k = len(ins), len(after), len(outs)

    def body(*refs):
        token = refs[n + m + k]
        token[...] = jnp.zeros(token.shape, F32)
        kernel(*refs[:n], *refs[n + m : n + m + k], *refs[n + m + k + 1 :])

    *got, token = pl.pallas_call(
        body,
        grid=(1,),
        out_shape=(*outs, shape((8, 128), F32)),
        in_specs=specs,
        out_specs=(*(out_specs or [vmem] * k), vmem),
        scratch_shapes=scratch,
        name=name,
        input_output_aliases=aliases or {},
        compiler_params=pltpu.CompilerParams(vmem_limit_bytes=40 * 1024 * 1024),
        cost_estimate=pl.CostEstimate(
            flops=int(COSTS.get(name, 1.0) * UNIT), bytes_accessed=1024, transcendentals=0
        ),
    )(*ins, *after)
    chain.append(token)
    return got


def shape(dims, kind):
    return jax.ShapeDtypeStruct(dims, kind)


def flatten_rows(src, scr, rows, columns, stride):
    for r in range(rows):
        scr[stride * r : stride * r + columns] = src[0, r].astype(F32)
        if stride > columns:
            scr[stride * r + columns : stride * (r + 1)] = jnp.zeros(
                (stride - columns, scr.shape[1]), F32
            )


def levels(parts):
    return parts.bit_length() - 1


def flip_bit(core, level, parts):
    return 1 << ((level + core) % levels(parts))


def owner(q, parts):
    core = lax.axis_index("dp") % 2
    at = lax.axis_index("space")
    for level in range(levels(parts)):
        if (q >> (levels(parts) - 1 - level)) & 1:
            at = at ^ jnp.where(core == 0, flip_bit(0, level, parts), flip_bit(1, level, parts))
    return at


def exchange(x, level, parts, dp):
    pairs = []
    for d in range(dp):
        for p in range(parts):
            pairs.append((d * parts + p, d * parts + (p ^ flip_bit(d % 2, level, parts))))
    return lax.ppermute(x, ("dp", "space"), pairs)


def split_kernel(dims, x_ref, *refs):
    rows, columns, stride, parts = dims
    outs, scr = refs[:parts], refs[parts]
    me = lax.axis_index("space")
    flatten_rows(x_ref, scr, rows, columns, stride)
    width = outs[0].shape[1]
    for b in range(parts):
        at = pl.multiple_of((me ^ b) * width, width)
        outs[b][...] = scr[:, pl.ds(at, width)].astype(BF)


def shifted_copies(pad_scr, half_scr, out, columns, stride, shifts):
    total, n = out.shape[0], pad_scr.shape[1]
    pad = (pad_scr.shape[0] - total) // 2
    limit = pad_scr.shape[0] - 8
    half_scr[0:limit] = pad_scr[4 : limit + 4]
    step = 2 * stride
    col = lax.broadcasted_iota(jnp.int32, (step, n), 0)
    col = jnp.where(col >= stride, col - stride, col)

    @pl.loop(0, total // step)
    def _(p):
        base = pl.multiple_of(p * step, step)
        for j, shift in enumerate(shifts):
            off = pad + shift
            if off % 8 == 0:
                v = pad_scr[pl.ds(pl.multiple_of(base + off, 8), step)]
            else:
                v = half_scr[pl.ds(pl.multiple_of(base + off - 4, 8), step)]
            if shift:
                ok = (col + shift >= 0) & (col + shift < columns)
                v = jnp.where(ok, v, 0.0)
            out[pl.ds(base, step), j * n : (j + 1) * n] = v.astype(BF)


def gather_blocks(blocks, pad_scr, pad):
    me = lax.axis_index("space")
    size, n = blocks[0].shape
    total = size * len(blocks)
    pad_scr[0:pad] = jnp.zeros((pad, n), F32)
    pad_scr[pad + total : 2 * pad + total] = jnp.zeros((pad, n), F32)
    for b, block in enumerate(blocks):
        at = pl.multiple_of((me ^ b) * size + pad, 8)
        pad_scr[pl.ds(at, size)] = block[...].astype(F32)


def mm(a, b, ca=1, cb=0):
    return lax.dot_general(a, b, (((ca,), (cb,)), ((), ())), preferred_element_type=F32)


def take_rows(scr, places, size, parts):
    rows = [scr[pl.ds(pl.multiple_of(owner(q, parts) * size, 8), size)] for q in places]
    return jnp.concatenate(rows, axis=0)


def forward_kernel(dims, branch, parts, w_ref, *refs):
    columns, stride = dims
    blocks, outs = refs[:parts], refs[parts:-6]
    pad_scr, half_scr, stack, acc, taps, sem = refs[-6:]
    copy = pltpu.make_async_copy(w_ref.at[branch], taps, sem)
    copy.start()
    spacing = dilations[branch]
    total = acc.shape[0]
    n = blocks[0].shape[1]
    gather_blocks(blocks, pad_scr, stride)
    shifted_copies(pad_scr, half_scr, stack, columns, stride, (-spacing, 0, spacing))
    copy.wait()
    step = spacing * stride
    w = [taps[3 * a : 3 * a + 3].reshape(3 * n, taps.shape[2]) for a in range(3)]
    acc[...] = mm(stack[...], w[1])
    acc[step:] += mm(stack[: total - step], w[0])
    acc[: total - step] += mm(stack[step:], w[2])
    keep, send = outs[:2]
    size = blocks[0].shape[0]
    keep[...] = take_rows(acc, range(parts // 2), size, parts)
    send[...] = take_rows(acc, range(parts // 2, parts), size, parts).astype(BF)
    if len(outs) > 2:
        outs[2][...] = stack[:, n : 2 * n]


def add_half_kernel(kept, got, keep, send):
    x = kept[...] + got[...].astype(F32)
    size = keep.shape[0]
    keep[...] = x[:size]
    send[...] = x[size:].astype(BF)


def join_rows_kernel(a, b, out):
    out[...] = jnp.concatenate([a[...].astype(F32), b[...].astype(F32)], axis=0).astype(BF)


def act_kernel(dims, branch, kept, got, bias_ref, go_ref, act_ref, grad_ref, scr):
    rows, columns, stride = dims
    flatten_rows(go_ref, scr, rows, columns, stride)
    pre = kept[...] + got[...].astype(F32) + bias_ref[branch : branch + 1, :]
    squash = jax.nn.sigmoid(pre)
    slope = squash * (1.0 + pre * (1.0 - squash))
    grad_ref[...] = (scr[...] * slope).astype(BF)
    scr[...] = pre * squash
    for r in range(rows):
        act_ref[0, r] = scr[stride * r : stride * r + columns].astype(BF)


def weight_kernel(dims, spacing, parts, mine, theirs, feat, keep, *refs):
    columns, stride = dims
    send, gstack, gpad, ghalf, full = refs
    core = lax.axis_index("dp") % 2
    total = gstack.shape[0]
    outputs = gpad.shape[1]
    size = total // parts
    gpad[0:stride] = jnp.zeros((stride, outputs), F32)
    gpad[stride + total :] = jnp.zeros((stride, outputs), F32)
    for q in range(parts):
        block = (mine, theirs)[2 * q // parts][...].astype(F32)
        at = q % (parts // 2) * size
        to = pl.multiple_of(owner(q, parts) * size + stride, 8)
        gpad[pl.ds(to, size)] = block[at : at + size]
    shifted_copies(gpad, ghalf, gstack, columns, stride, (spacing, 0, -spacing))
    step = spacing * stride
    for a in range(3):
        if a == 0:
            f, g = feat[: total - step], gstack[step:]
        elif a == 1:
            f, g = feat[...], gstack[...]
        else:
            f, g = feat[step:], gstack[: total - step]
        r = mm(f, g, 0, 0)
        for c in range(3):
            full[3 * a + c] = r[:, c * outputs : (c + 1) * outputs]
    half = full.shape[1] // 2
    body = 9 * half
    own = full[:, pl.ds(pl.multiple_of(core * half, half), half)]
    other = full[:, pl.ds(pl.multiple_of((1 - core) * half, half), half)]
    keep[:body] = own.reshape(body, outputs)
    send[:body] = other.reshape(body, outputs).astype(BF)
    total_bias = jnp.sum(gpad[...], axis=0, keepdims=True)
    row = lax.broadcasted_iota(jnp.int32, (EXTRA, outputs), 0)
    own_bias = jnp.where(row == 0, total_bias, 0.0)
    keep[body:] = own_bias
    send[body:] = pack_extra(own_bias)


def pack_extra(x):
    total = jnp.sum(x, axis=0, keepdims=True)
    high = total.astype(BF).astype(F32)
    row = lax.broadcasted_iota(jnp.int32, x.shape, 0)
    return jnp.where(row == 0, high, jnp.where(row == 1, total - high, 0.0)).astype(BF)


def add_pack_kernel(body, *refs):
    ins, out_ref = refs[:-1], refs[-1]
    end = body + EXTRA
    total = ins[0][:end].astype(F32)
    for x in ins[1:]:
        total = total + x[:end].astype(F32)
    out_ref[:body] = total[:body].astype(BF)
    out_ref[body:end] = pack_extra(total[body:])
    if out_ref.shape[0] > end:
        out_ref[end:] = jnp.zeros((out_ref.shape[0] - end, out_ref.shape[1]), BF)


def put_half(x, out, buf, sem, place, at, scale):
    half, outputs = buf.shape[1:]
    buf[...] = (x[: 9 * half].astype(F32) * scale).reshape(9, half, outputs)
    rows = pl.ds(pl.multiple_of(at * half, half), half)
    copy = pltpu.make_async_copy(buf, out.at[place, :, rows], sem)
    copy.start()
    return copy


def choose_kernel(scale, place, lined, *refs):
    inner = refs[0][...]
    if lined:
        chip = lax.axis_index("dp") // 2
        inner = jnp.where((chip == 1) | (chip == 2), inner, refs[1][...])
    outs = refs[2 if lined else 1 :]
    if place is None:
        outs[0][...] = inner
        return
    own, out, buf, sem = outs[-4:]
    own[...] = inner
    put_half(inner, out, buf, sem, place, lax.axis_index("dp") % 2, scale).wait()


def weight_out_kernel(scale, halves, *refs):
    n = len(halves)
    out, bufs, sems = refs[-3:]
    core = lax.axis_index("dp") % 2
    copies = []
    for i, (place, own) in enumerate(halves):
        at = core if own else 1 - core
        copies.append(put_half(refs[i], out, bufs.at[i], sems.at[i], place, at, scale))
    for copy in copies:
        copy.wait()


def bias_kernel(scale, body, ins, out):
    for k, x in enumerate(ins):
        total = jnp.sum(x[body : body + EXTRA].astype(F32), axis=0, keepdims=True)
        out[k : k + 1, :] = total * scale


def touch_kernel(w_ref):
    pass


def input_kernel(dims, parts, w_ref, *refs):
    stacks = refs[:3]
    acc, taps, sem = refs[3:]
    copy = pltpu.make_async_copy(w_ref, taps, sem)
    copy.start()
    copy.wait()
    total = acc.shape[0]
    for k, spacing in enumerate(dilations):
        g = stacks[k]
        step = spacing * dims[1]
        for a in (1, 0, 2):
            w = jnp.concatenate([taps[k, 3 * a + c] for c in range(3)], axis=1)
            if a == 1:
                r = mm(g[...], w, 1, 1)
                if k == 0:
                    acc[...] = r
                else:
                    acc[...] += r
            elif a == 0:
                acc[: total - step] += mm(g[step:], w, 1, 1)
            else:
                acc[step:] += mm(g[: total - step], w, 1, 1)


def split_rows_kernel(parts, acc, *outs):
    me = lax.axis_index("space")
    size = outs[0].shape[0]
    for b in range(parts):
        at = pl.multiple_of((me ^ b) * size, 8)
        outs[b][...] = acc[pl.ds(at, size)].astype(BF)


def join_kernel(dims, parts, *refs):
    rows, columns, stride = dims
    blocks, out_ref, scr = refs[:parts], refs[parts], refs[parts + 1]
    me = lax.axis_index("space")
    width = blocks[0].shape[1]
    for b in range(parts):
        at = pl.multiple_of((me ^ b) * width, width)
        scr[:, pl.ds(at, width)] = blocks[b][...].astype(F32)
    for r in range(rows):
        out_ref[0, r] = scr[stride * r : stride * r + columns].astype(BF)


def merge_kernel(*refs):
    ins, out = refs[:-1], refs[-1]
    n = ins[0].shape[3]
    for k, x in enumerate(ins):
        out[:, :, :, k * n : (k + 1) * n] = x[...]


def swap(x, bit):
    n = lax.axis_size("space")
    return lax.ppermute(x, "space", [(i, i ^ bit) for i in range(n)])


def per_device(features, weights, bias, grad_out):
    images, rows, columns, channels_all = features.shape
    assert images == 1
    parts = lax.axis_size("space")
    dp = lax.axis_size("dp")
    channels, outputs = weights.shape[2], weights.shape[3]
    stride = stride_of(columns)
    size = rows * stride
    total = size * parts
    padded = total + 2 * stride
    vm = pltpu.VMEM
    whole = pl.BlockSpec(memory_space=pltpu.VMEM)
    far = pl.BlockSpec(memory_space=pltpu.HBM)
    top = levels(parts)
    cores = [(i, i ^ 1) for i in range(dp)]
    half = channels // 2
    kept_rows = 9 * half + EXTRA
    packed = [shape((kept_rows + 16, outputs), BF)]
    chain = []
    run = functools.partial(call, chain)

    mine = run(
        functools.partial(split_kernel, (rows, columns, stride, parts)),
        [features],
        [shape((size, channels), BF)] * parts,
        [vm((size, channels_all), F32)],
        "split_channels",
    )
    feats = [mine[0]] + [swap(mine[b], b) for b in range(1, parts)]

    state = {}
    rows_kept = size * parts // 2

    def forward(k, with_feat=False):
        outs = [shape((rows_kept, outputs), F32), shape((rows_kept, outputs), BF)]
        if with_feat:
            outs.append(shape((total, channels), BF))
        got = run(
            functools.partial(forward_kernel, (columns, stride), k, parts),
            [weights] + feats,
            outs,
            [
                vm((padded, channels), F32),
                vm((padded, channels), F32),
                vm((total, 3 * channels), BF),
                vm((total, outputs), F32),
                vm((9, channels, outputs), BF),
                pltpu.SemaphoreType.DMA,
            ],
            f"forward_{k}",
            in_specs=[far] + [whole] * parts,
        )
        if with_feat:
            state["feat"] = got[2]
        state[k] = (got[0], exchange(got[1], 0, parts, dp))

    def reduce_step(k, level):
        keep, got = state[k]
        n = keep.shape[0] // 2
        outs = [shape((n, outputs), F32), shape((n, outputs), BF)]
        keep, send = run(add_half_kernel, [keep, got], outs, [], f"add_{k}")
        state[k] = (keep, exchange(send, level, parts, dp))

    def activate(k):
        keep, got = state[k]
        act, grad = run(
            functools.partial(act_kernel, (rows, columns, stride), k),
            [keep, got, bias, grad_out],
            [shape((1, rows, columns, outputs), BF), shape((size, outputs), BF)],
            [vm((size, outputs), F32)],
            f"activation_{k}",
            in_specs=[whole] * 3 + [pl.BlockSpec((1, rows, columns, outputs), lambda i: (0, 0, 0, k))],
        )
        state[k] = (grad, exchange(grad, top - 1, parts, dp))
        state["act", k] = act

    def gather_step(k, level):
        own, got = state[k]
        outs = [shape((2 * own.shape[0], outputs), BF)]
        both = run(join_rows_kernel, [own, got], outs, [], f"join_{k}")[0]
        state[k] = (both, exchange(both, level, parts, dp))

    def weight_part(k):
        own, got = state[k]
        keep, send, stack = run(
            functools.partial(weight_kernel, (columns, stride), dilations[k], parts),
            [own, got, state["feat"]],
            [
                shape((kept_rows, outputs), F32),
                shape((kept_rows, outputs), BF),
                shape((total, 3 * outputs), BF),
            ],
            [
                vm((padded, outputs), F32),
                vm((padded, outputs), F32),
                vm((9, channels, outputs), F32),
            ],
            f"weight_grad_{k}",
        )
        state["stack", k] = stack
        state["sum", k] = [keep, lax.ppermute(send, "dp", cores)]

    def line(pairs):
        return [(2 * a + c, 2 * b + c) for a, b in pairs for c in range(2)]

    def add(name, ins):
        return run(functools.partial(add_pack_kernel, 9 * half), ins, packed, [], name)[0]

    def add_cores(k):
        got = state["sum", k]
        if dp != 8:
            kept = got[0] + got[1].astype(F32)
            groups = [[2 * i + c for i in range(dp // 2)] for c in range(2)]
            state["sum", k] = lax.psum(kept, "dp", axis_index_groups=groups)
            return
        near = add(f"add_cores_{k}", got)
        state["sum", k] = got + [lax.ppermute(near, "dp", line([(0, 1), (3, 2)]))]

    def add_near(k):
        if dp == 8:
            near = add(f"add_near_{k}", state["sum", k])
            state["sum", k] = [near, lax.ppermute(near, "dp", line([(1, 2), (2, 1)]))]

    def add_far(k):
        if dp != 8:
            state["sum", k] = [add(f"round_{k}", [state["sum", k]])]
            return
        far_sum = add(f"add_far_{k}", state["sum", k])
        state["sum", k] = [far_sum, lax.ppermute(far_sum, "dp", line([(1, 0), (2, 3)]))]

    anywhere = pl.BlockSpec(memory_space=pl.ANY)
    weight_shape = shape((3, 9, channels, outputs), F32)

    def choose(k, last=False):
        ins = state["sum", k]
        place, outs, scratch, specs, out_specs, aliases = None, packed, [], None, None, None
        if not last:
            place, outs = k, packed + [weight_shape]
            scratch = [vm((9, half, outputs), F32), pltpu.SemaphoreType.DMA]
            out_specs = [whole, anywhere]
            if "weight_grad" in state:
                ins = ins + [state["weight_grad"]]
                specs = [whole] * (len(ins) - 1) + [anywhere]
                aliases = {len(ins) - 1: 1}
        got = run(
            functools.partial(choose_kernel, 1.0 / dp, place, dp == 8),
            ins,
            outs,
            scratch,
            f"choose_{k}",
            in_specs=specs,
            out_specs=out_specs,
            aliases=aliases,
        )
        if not last:
            state["weight_grad"] = got[1]
        state["own", k] = got[0]
        state["sum", k] = lax.ppermute(got[0], "dp", cores)

    def weight_out(name, halves, with_bias=False):
        ins = [state["own" if own else "sum", k] for k, own in halves]
        n = len(ins)
        extra = [state["own", k] for k in range(3)] if with_bias else []
        outs = [weight_shape] + ([shape((3, outputs), F32)] if with_bias else [])

        def kernel(*refs):
            if with_bias:
                bias_kernel(1.0 / dp, 9 * half, refs[n : n + 3], refs[-3])
                refs = (*refs[: -3], *refs[-2:])
            weight_out_kernel(1.0 / dp, halves, *refs[:n], refs[-3], *refs[-2:])

        got = run(
            kernel,
            ins + extra + [state["weight_grad"]],
            outs,
            [vm((n, 9, half, outputs), F32), pltpu.SemaphoreType.DMA((n,))],
            name,
            in_specs=[whole] * (n + len(extra)) + [anywhere],
            out_specs=[anywhere] + [whole] * (len(outs) - 1),
            aliases={n + len(extra): 0},
        )
        state["weight_grad"] = got[0]
        return got[-1]

    def input_part():
        state["back"] = run(
            functools.partial(input_kernel, (columns, stride), parts),
            [weights] + [state["stack", k] for k in range(3)],
            [shape((total, channels), F32)],
            [vm(weights.shape, BF), pltpu.SemaphoreType.DMA],
            "input_grad",
            in_specs=[far] + [whole] * 3,
        )

    def send_back():
        outs = [shape((size, channels), BF)] * parts
        back = run(functools.partial(split_rows_kernel, parts), state["back"], outs, [], "split_rows")
        state["back"] = [back[0]] + [swap(back[b], b) for b in range(1, parts)]

    def join_back():
        state["input_grad"] = run(
            functools.partial(join_kernel, (rows, columns, stride), parts),
            state["back"],
            [shape(features.shape, BF)],
            [vm((size, channels_all), F32)],
            "join_channels",
        )[0]

    def merge():
        acts = [state["act", k] for k in range(3)]
        state["active"] = run(
            merge_kernel, acts, [shape(grad_out.shape, BF)], [], "merge_branches"
        )[0]

    k0, k1, k2 = 2, 0, 1
    run(touch_kernel, [weights], [], [], "touch_weights", in_specs=[far])
    forward(k0, with_feat=True)
    forward(k1)
    if top == 2:
        reduce_step(k0, 1)
        forward(k2)
        reduce_step(k1, 1)
        activate(k0)
        reduce_step(k2, 1)
        activate(k1)
        gather_step(k0, 0)
        activate(k2)
        gather_step(k1, 0)
        weight_part(k0)
        gather_step(k2, 0)
        add_cores(k0)
        weight_part(k1)
        weight_part(k2)
        add_cores(k1)
        add_cores(k2)
        add_near(k0)
        input_part()
        send_back()
        add_near(k1)
        add_far(k0)
        add_near(k2)
        add_far(k1)
        choose(k0)
        add_far(k2)
    else:
        forward(k2)
        for k in (k0, k1, k2):
            for level in range(1, top):
                reduce_step(k, level)
            activate(k)
            for level in range(top - 2, -1, -1):
                gather_step(k, level)
            weight_part(k)
            add_cores(k)
            add_near(k)
        input_part()
        send_back()
        add_far(k0)
        add_far(k1)
        choose(k0)
        add_far(k2)
    merge()
    join_back()
    choose(k1)
    choose(k2, last=True)
    weight_out("weight_out_a", [(k0, False), (k1, False)])
    bias_grad = weight_out("weight_out_b", [(k2, False), (k2, True)], with_bias=True)
    return state["active"], state["input_grad"], state["weight_grad"], bias_grad


def solution(mesh):
    placed = (
        P("dp", "space", None, None),
        P(None, None, "space", None),
        P(),
        P("dp", "space", None, None),
    )
    return jax.shard_map(
        per_device,
        mesh=mesh,
        in_specs=placed,
        out_specs=(
            P("dp", "space", None, None),
            P("dp", "space", None, None),
            P(None, None, "space", None),
            P(),
        ),
        check_vma=False,
    )
```

```python
import functools

import jax
import jax.numpy as jnp
from jax import lax
from jax.experimental import pallas as pl
from jax.experimental.pallas import tpu as pltpu
from jax.sharding import PartitionSpec as P

dilations = (12, 24, 36)
BF = jnp.bfloat16
F32 = jnp.float32
EXTRA = 16


def stride_of(columns):
    return -(-columns // 8) * 8


COSTS = {"input_grad": 0.05, "add_near_0": 0.05, "add_near_2": 0.05, "add_near_1": 0, "split_rows": 0.05, "add_far_0": 0.05, "add_far_2": 0.05, "add_far_1": 0.05, "merge_branches": 0.05, "join_channels": 0.05, "choose_0": 0.05, "choose_2": 0.05, "choose_1": 0.05, "weight_out_a": 0.05, "weight_out_b": 0.05, "add_cores_1": 1, "join_2": 3, "add_cores_0": 0, "add_cores_2": 0, "weight_grad_2": 0, "pass_on": 0.05, "weight_out_c": 0.05}
UNIT = 1_150_000_000


def call(
    chain, kernel, ins, outs, scratch, name, in_specs=None, out_specs=None, aliases=None, last=False
):
    after = chain[-1:]
    vmem = pl.BlockSpec(memory_space=pltpu.VMEM)
    specs = list(in_specs or [vmem] * len(ins)) + [pl.BlockSpec(memory_space=pl.ANY)] * len(after)
    n, m, k = len(ins), len(after), len(outs)

    def body(*refs):
        rest = refs[n + m + k :]
        if not last:
            rest[0][...] = jnp.zeros(rest[0].shape, F32)
            rest = rest[1:]
        kernel(*refs[:n], *refs[n + m : n + m + k], *rest)

    got = pl.pallas_call(
        body,
        grid=(1,),
        out_shape=(*outs, *([] if last else [shape((8, 128), F32)])),
        in_specs=specs,
        out_specs=(*(out_specs or [vmem] * k), *([] if last else [vmem])),
        scratch_shapes=scratch,
        name=name,
        input_output_aliases=aliases or {},
        compiler_params=pltpu.CompilerParams(vmem_limit_bytes=40 * 1024 * 1024),
        cost_estimate=pl.CostEstimate(
            flops=int(COSTS.get(name, 1.0) * UNIT), bytes_accessed=1024, transcendentals=0
        ),
    )(*ins, *after)
    if last:
        return list(got)
    chain.append(got[-1])
    return list(got[:-1])


def shape(dims, kind):
    return jax.ShapeDtypeStruct(dims, kind)


def flatten_rows(src, scr, rows, columns, stride):
    for r in range(rows):
        scr[stride * r : stride * r + columns] = src[0, r].astype(F32)
        if stride > columns:
            scr[stride * r + columns : stride * (r + 1)] = jnp.zeros(
                (stride - columns, scr.shape[1]), F32
            )


def levels(parts):
    return parts.bit_length() - 1


def flip_bit(core, level, parts):
    return 1 << ((level + core) % levels(parts))


def owner(q, parts):
    core = lax.axis_index("dp") % 2
    at = lax.axis_index("space")
    for level in range(levels(parts)):
        if (q >> (levels(parts) - 1 - level)) & 1:
            at = at ^ jnp.where(core == 0, flip_bit(0, level, parts), flip_bit(1, level, parts))
    return at


def exchange(x, level, parts, dp):
    pairs = []
    for d in range(dp):
        for p in range(parts):
            pairs.append((d * parts + p, d * parts + (p ^ flip_bit(d % 2, level, parts))))
    return lax.ppermute(x, ("dp", "space"), pairs)


def split_kernel(dims, x_ref, *refs):
    rows, columns, stride, parts = dims
    outs, scr = refs[:parts], refs[parts]
    me = lax.axis_index("space")
    flatten_rows(x_ref, scr, rows, columns, stride)
    width = outs[0].shape[1]
    for b in range(parts):
        at = pl.multiple_of((me ^ b) * width, width)
        outs[b][...] = scr[:, pl.ds(at, width)].astype(BF)


def shifted_copies(pad_scr, half_scr, out, columns, stride, shifts):
    total, n = out.shape[0], pad_scr.shape[1]
    pad = (pad_scr.shape[0] - total) // 2
    limit = pad_scr.shape[0] - 8
    half_scr[0:limit] = pad_scr[4 : limit + 4]
    step = 2 * stride
    col = lax.broadcasted_iota(jnp.int32, (step, n), 0)
    col = jnp.where(col >= stride, col - stride, col)

    @pl.loop(0, total // step)
    def _(p):
        base = pl.multiple_of(p * step, step)
        for j, shift in enumerate(shifts):
            off = pad + shift
            if off % 8 == 0:
                v = pad_scr[pl.ds(pl.multiple_of(base + off, 8), step)]
            else:
                v = half_scr[pl.ds(pl.multiple_of(base + off - 4, 8), step)]
            if shift:
                ok = (col + shift >= 0) & (col + shift < columns)
                v = jnp.where(ok, v, 0.0)
            out[pl.ds(base, step), j * n : (j + 1) * n] = v.astype(BF)


def gather_blocks(blocks, pad_scr, pad):
    me = lax.axis_index("space")
    size, n = blocks[0].shape
    total = size * len(blocks)
    pad_scr[0:pad] = jnp.zeros((pad, n), F32)
    pad_scr[pad + total : 2 * pad + total] = jnp.zeros((pad, n), F32)
    for b, block in enumerate(blocks):
        at = pl.multiple_of((me ^ b) * size + pad, 8)
        pad_scr[pl.ds(at, size)] = block[...].astype(F32)


def mm(a, b, ca=1, cb=0):
    return lax.dot_general(a, b, (((ca,), (cb,)), ((), ())), preferred_element_type=F32)


def take_rows(scr, places, size, parts):
    rows = [scr[pl.ds(pl.multiple_of(owner(q, parts) * size, 8), size)] for q in places]
    return jnp.concatenate(rows, axis=0)


def forward_kernel(dims, branch, parts, w_ref, *refs):
    columns, stride = dims
    blocks, outs = refs[:parts], refs[parts:-6]
    pad_scr, half_scr, stack, acc, taps, sem = refs[-6:]
    copy = pltpu.make_async_copy(w_ref.at[branch], taps, sem)
    copy.start()
    spacing = dilations[branch]
    total = acc.shape[0]
    n = blocks[0].shape[1]
    gather_blocks(blocks, pad_scr, stride)
    shifted_copies(pad_scr, half_scr, stack, columns, stride, (-spacing, 0, spacing))
    copy.wait()
    step = spacing * stride
    w = [taps[3 * a : 3 * a + 3].reshape(3 * n, taps.shape[2]) for a in range(3)]
    acc[...] = mm(stack[...], w[1])
    acc[step:] += mm(stack[: total - step], w[0])
    acc[: total - step] += mm(stack[step:], w[2])
    keep, send = outs[:2]
    size = blocks[0].shape[0]
    keep[...] = take_rows(acc, range(parts // 2), size, parts)
    send[...] = take_rows(acc, range(parts // 2, parts), size, parts).astype(BF)
    if len(outs) > 2:
        outs[2][...] = stack[:, n : 2 * n]


def add_half_kernel(kept, got, keep, send):
    x = kept[...] + got[...].astype(F32)
    size = keep.shape[0]
    keep[...] = x[:size]
    send[...] = x[size:].astype(BF)


def join_rows_kernel(a, b, out):
    out[...] = jnp.concatenate([a[...].astype(F32), b[...].astype(F32)], axis=0).astype(BF)


def act_kernel(dims, branch, kept, got, bias_ref, go_ref, act_ref, grad_ref, scr):
    rows, columns, stride = dims
    flatten_rows(go_ref, scr, rows, columns, stride)
    pre = kept[...] + got[...].astype(F32) + bias_ref[branch : branch + 1, :]
    squash = jax.nn.sigmoid(pre)
    slope = squash * (1.0 + pre * (1.0 - squash))
    grad_ref[...] = (scr[...] * slope).astype(BF)
    scr[...] = pre * squash
    for r in range(rows):
        act_ref[0, r] = scr[stride * r : stride * r + columns].astype(BF)


def corner_rows(slab, rows, stride, column):
    return jnp.concatenate([slab[stride * r + column : stride * r + column + 1] for r in range(rows)])


def in_slot(x, slots):
    row = lax.broadcasted_iota(jnp.int32, (slots * x.shape[0], x.shape[1]), 0)
    mine = row // x.shape[0] == lax.axis_index("dp")
    return jnp.where(mine, jnp.concatenate([x] * slots), 0.0)


def weight_kernel(dims, spacing, parts, near, mine, theirs, feat, keep, *refs):
    columns, stride = dims
    send, gstack, gpad, ghalf, full = refs
    core = lax.axis_index("dp") % 2
    total = gstack.shape[0]
    outputs = gpad.shape[1]
    gpad[0:stride] = jnp.zeros((stride, outputs), F32)
    gpad[stride + total :] = jnp.zeros((stride, outputs), F32)
    size = total // parts
    for q in range(parts):
        block = (mine, theirs)[2 * q // parts][...].astype(F32)
        at = q % (parts // 2) * size
        to = pl.multiple_of(owner(q, parts) * size + stride, 8)
        gpad[pl.ds(to, size)] = block[at : at + size]
    shifted_copies(gpad, ghalf, gstack, columns, stride, (spacing, 0, -spacing))
    step = spacing * stride
    at = 0
    for a in range(3):
        if a == 0:
            f, g = feat[: total - step], gstack[step:]
        elif a == 1:
            f, g = feat[...], gstack[...]
        else:
            f, g = feat[step:], gstack[: total - step]
        taps = (1,) if near and a != 1 else (0, 1, 2)
        if len(taps) == 1:
            g = g[:, outputs : 2 * outputs]
        r = mm(f, g, 0, 0)
        for c in range(len(taps)):
            full[at + c] = r[:, c * outputs : (c + 1) * outputs]
        at += len(taps)
    half = full.shape[1] // 2
    body = at * half
    own = full[:at, pl.ds(pl.multiple_of(core * half, half), half)]
    other = full[:at, pl.ds(pl.multiple_of((1 - core) * half, half), half)]
    keep[:body] = own.reshape(body, outputs)
    send[:body] = other.reshape(body, outputs).astype(BF)
    total_bias = jnp.sum(gpad[...], axis=0, keepdims=True)
    row = lax.broadcasted_iota(jnp.int32, (EXTRA, outputs), 0)
    own_bias = jnp.where(row == 0, total_bias, 0.0)
    keep[body : body + EXTRA] = own_bias
    send[body : body + EXTRA] = pack_extra(own_bias)
    if near:
        slots = lax.axis_size("dp")
        ends = (0, total - near * stride)
        last = columns - 1
        fs = [feat[e : e + near * stride].astype(F32) for e in ends]
        gs = [gpad[stride + e : stride + e + near * stride] for e in ends]
        at, n = body + EXTRA, near * slots
        for a in range(2):
            for c in range(2):
                f = in_slot(corner_rows(fs[a], near, stride, c * last), slots)
                g = in_slot(corner_rows(gs[1 - a], near, stride, (1 - c) * last), slots)
                first = core == 0
                keep[at : at + n] = jnp.where(first, f[:, :half], f[:, half:])
                send[at : at + n] = jnp.where(first, f[:, half:], f[:, :half]).astype(BF)
                keep[at + 4 * n : at + 5 * n] = g
                send[at + 4 * n : at + 5 * n] = g.astype(BF)
                at += n


def pack_extra(x):
    total = jnp.sum(x, axis=0, keepdims=True)
    high = total.astype(BF).astype(F32)
    row = lax.broadcasted_iota(jnp.int32, x.shape, 0)
    return jnp.where(row == 0, high, jnp.where(row == 1, total - high, 0.0)).astype(BF)


def add_pack_kernel(body, *refs):
    ins, out_ref = refs[:-1], refs[-1]
    n = ins[0].shape[0]
    for x in ins:
        n = min(n, x.shape[0])
    total = ins[0][:n].astype(F32)
    for x in ins[1:]:
        total = total + x[:n].astype(F32)
    out_ref[:n] = total.astype(BF)
    out_ref[body : body + EXTRA] = pack_extra(total[body : body + EXTRA])
    if out_ref.shape[0] > n:
        out_ref[n:] = jnp.zeros((out_ref.shape[0] - n, out_ref.shape[1]), BF)


def put_half(x, near, out, buf, sems, place, at, scale):
    half, outputs = buf.shape[1:]
    rows = pl.ds(pl.multiple_of(at * half, half), half)
    copies = []

    def send(first, count):
        sem = sems.at[len(copies)]
        src, dst = buf.at[first : first + count], out.at[place, first : first + count, rows]
        copies.append(pltpu.make_async_copy(src, dst, sem))
        copies[-1].start()

    if not near:
        for a in range(3):
            part = x[3 * a * half : 3 * (a + 1) * half].astype(F32) * scale
            buf[3 * a : 3 * a + 3] = part.reshape(3, half, outputs)
            send(3 * a, 3)
        return copies
    i = 0
    for first, count in ((1, 1), (3, 3), (7, 1)):
        part = x[i * half : (i + count) * half].astype(F32) * scale
        buf[first : first + count] = part.reshape(count, half, outputs)
        send(first, count)
        i += count
    n = near * lax.axis_size("dp")
    start = 5 * half + EXTRA
    f, g = x[start : start + 4 * n], x[start + 4 * n : start + 8 * n].astype(F32)
    corner = lax.broadcasted_iota(jnp.int32, g.shape, 0) // n
    spread = jnp.concatenate([jnp.where(corner == i, g, 0.0) for i in range(4)], axis=1)
    r = mm(f, spread.astype(BF), 0, 0) * scale
    for i, t in enumerate((0, 2, 6, 8)):
        buf[t] = r[:, i * outputs : (i + 1) * outputs]
        send(t, 1)
    return copies


def choose_kernel(scale, place, lined, *refs):
    inner = refs[0][...]
    if lined:
        chip = lax.axis_index("dp") // 2
        inner = jnp.where((chip == 1) | (chip == 2), inner, refs[1][...])
    outs = refs[2 if lined else 1 :]
    if place is None:
        outs[0][...] = inner
        return
    own, out, buf, sem = outs[-4:]
    own[...] = inner
    for copy in put_half(inner, 0, out, buf, sem, place, lax.axis_index("dp") % 2, scale):
        copy.wait()


def weight_out_kernel(scale, halves, *refs):
    n = len(halves)
    out, bufs, sems = refs[-3:]
    core = lax.axis_index("dp") % 2
    copies = []
    for i, (place, own, near) in enumerate(halves):
        at = core if own else 1 - core
        copies += put_half(refs[i], near, out, bufs.at[i], sems.at[i], place, at, scale)
    for copy in copies:
        copy.wait()


def bias_kernel(scale, bodies, ins, out):
    for k, x in enumerate(ins):
        body = bodies[k]
        total = jnp.sum(x[body : body + EXTRA].astype(F32), axis=0, keepdims=True)
        out[k : k + 1, :] = total * scale


def touch_kernel(w_ref):
    pass


def input_kernel(dims, parts, w_ref, *refs):
    stacks = refs[:3]
    acc, taps, sem = refs[3:]
    copy = pltpu.make_async_copy(w_ref, taps, sem)
    copy.start()
    copy.wait()
    total = acc.shape[0]
    for k, spacing in enumerate(dilations):
        g = stacks[k]
        step = spacing * dims[1]
        for a in (1, 0, 2):
            w = jnp.concatenate([taps[k, 3 * a + c] for c in range(3)], axis=1)
            if a == 1:
                r = mm(g[...], w, 1, 1)
                if k == 0:
                    acc[...] = r
                else:
                    acc[...] += r
            elif a == 0:
                acc[: total - step] += mm(g[step:], w, 1, 1)
            else:
                acc[step:] += mm(g[: total - step], w, 1, 1)


def split_rows_kernel(parts, acc, *outs):
    size = acc.shape[0] // parts
    if len(outs) == 3:
        outs[0][...] = take_rows(acc, [0], size, parts).astype(BF)
        outs[1][...] = take_rows(acc, [1], size, parts).astype(BF)
        outs[2][...] = take_rows(acc, [2, 3], size, parts).astype(BF)
        return
    me = lax.axis_index("space")
    for b in range(parts):
        at = pl.multiple_of((me ^ b) * size, 8)
        outs[b][...] = acc[pl.ds(at, size)].astype(BF)


def pass_on_kernel(own, got, out):
    size = own.shape[0]
    out[:size] = own[...]
    out[size:] = got[size:]


def join_kernel(dims, parts, *refs):
    rows, columns, stride = dims
    blocks, out_ref, scr = refs[:-2], refs[-2], refs[-1]
    me = lax.axis_index("space")
    width, size = blocks[0].shape[1], scr.shape[0]
    if len(blocks) == 3:
        parted = [(blocks[0], 0), (blocks[2], 0), (blocks[1], 0), (blocks[2], 1)]
        places = [owner(q, parts) for q in range(4)]
    else:
        parted = [(block, 0) for block in blocks]
        places = [me ^ b for b in range(parts)]
    for (block, n), place in zip(parted, places):
        at = pl.multiple_of(place * width, width)
        scr[:, pl.ds(at, width)] = block[n * size : (n + 1) * size].astype(F32)
    for r in range(rows):
        out_ref[0, r] = scr[stride * r : stride * r + columns].astype(BF)


def merge_kernel(*refs):
    ins, out = refs[:-1], refs[-1]
    n = ins[0].shape[3]
    for k, x in enumerate(ins):
        out[:, :, :, k * n : (k + 1) * n] = x[...]


def swap(x, bit):
    n = lax.axis_size("space")
    return lax.ppermute(x, "space", [(i, i ^ bit) for i in range(n)])


def per_device(features, weights, bias, grad_out):
    images, rows, columns, channels_all = features.shape
    assert images == 1
    parts = lax.axis_size("space")
    dp = lax.axis_size("dp")
    channels, outputs = weights.shape[2], weights.shape[3]
    stride = stride_of(columns)
    size = rows * stride
    total = size * parts
    padded = total + 2 * stride
    vm = pltpu.VMEM
    whole = pl.BlockSpec(memory_space=pltpu.VMEM)
    far = pl.BlockSpec(memory_space=pltpu.HBM)
    top = levels(parts)
    cores = [(i, i ^ 1) for i in range(dp)]
    half = channels // 2
    near, body, kept_rows = [], [], []
    for spacing in dilations:
        few = rows * parts - spacing
        if dp == 8 and few == 4 and columns - spacing == 1 and half == outputs and size % 16 == 0:
            near.append(few)
            body.append(5 * half)
            kept_rows.append(5 * half + EXTRA + 8 * few * dp)
        else:
            near.append(0)
            body.append(9 * half)
            kept_rows.append(9 * half + EXTRA)

    def packed(k):
        return [shape((kept_rows[k] + 16, outputs), BF)]

    chain = []
    run = functools.partial(call, chain)

    mine = run(
        functools.partial(split_kernel, (rows, columns, stride, parts)),
        [features],
        [shape((size, channels), BF)] * parts,
        [vm((size, channels_all), F32)],
        "split_channels",
    )
    feats = [mine[0]] + [swap(mine[b], b) for b in range(1, parts)]

    state = {}
    rows_kept = size * parts // 2

    def forward(k, with_feat=False):
        outs = [shape((rows_kept, outputs), F32), shape((rows_kept, outputs), BF)]
        if with_feat:
            outs.append(shape((total, channels), BF))
        got = run(
            functools.partial(forward_kernel, (columns, stride), k, parts),
            [weights] + feats,
            outs,
            [
                vm((padded, channels), F32),
                vm((padded, channels), F32),
                vm((total, 3 * channels), BF),
                vm((total, outputs), F32),
                vm((9, channels, outputs), BF),
                pltpu.SemaphoreType.DMA,
            ],
            f"forward_{k}",
            in_specs=[far] + [whole] * parts,
        )
        if with_feat:
            state["feat"] = got[2]
        state[k] = (got[0], exchange(got[1], 0, parts, dp))

    def reduce_step(k, level):
        keep, got = state[k]
        n = keep.shape[0] // 2
        outs = [shape((n, outputs), F32), shape((n, outputs), BF)]
        keep, send = run(add_half_kernel, [keep, got], outs, [], f"add_{k}")
        state[k] = (keep, exchange(send, level, parts, dp))

    def activate(k):
        keep, got = state[k]
        act, grad = run(
            functools.partial(act_kernel, (rows, columns, stride), k),
            [keep, got, bias, grad_out],
            [shape((1, rows, columns, outputs), BF), shape((size, outputs), BF)],
            [vm((size, outputs), F32)],
            f"activation_{k}",
            in_specs=[whole] * 3 + [pl.BlockSpec((1, rows, columns, outputs), lambda i: (0, 0, 0, k))],
        )
        state[k] = (grad, exchange(grad, top - 1, parts, dp))
        state["act", k] = act

    def gather_step(k, level):
        own, got = state[k]
        outs = [shape((2 * own.shape[0], outputs), BF)]
        both = run(join_rows_kernel, [own, got], outs, [], f"join_{k}")[0]
        state[k] = (both, exchange(both, level, parts, dp))

    def weight_part(k):
        own, got = state[k]
        keep, send, stack = run(
            functools.partial(weight_kernel, (columns, stride), dilations[k], parts, near[k]),
            [own, got, state["feat"]],
            [
                shape((kept_rows[k], outputs), F32),
                shape((kept_rows[k], outputs), BF),
                shape((total, 3 * outputs), BF),
            ],
            [
                vm((padded, outputs), F32),
                vm((padded, outputs), F32),
                vm((9, channels, outputs), F32),
            ],
            f"weight_grad_{k}",
        )
        state["stack", k] = stack
        state["sum", k] = [keep, lax.ppermute(send, "dp", cores)]

    def line(pairs):
        return [(2 * a + c, 2 * b + c) for a, b in pairs for c in range(2)]

    def add(name, k, ins):
        kernel = functools.partial(add_pack_kernel, body[k])
        return run(kernel, ins, packed(k), [], f"{name}_{k}")[0]

    def add_cores(k):
        got = state["sum", k]
        if dp != 8:
            kept = got[0] + got[1].astype(F32)
            groups = [[2 * i + c for i in range(dp // 2)] for c in range(2)]
            state["sum", k] = lax.psum(kept, "dp", axis_index_groups=groups)
            return
        near = add("add_cores", k, got)
        state["sum", k] = got + [lax.ppermute(near, "dp", line([(0, 1), (3, 2)]))]

    def add_near(k):
        if dp == 8:
            near = add("add_near", k, state["sum", k])
            state["sum", k] = [near, lax.ppermute(near, "dp", line([(1, 2), (2, 1)]))]

    def add_far(k):
        if dp != 8:
            state["sum", k] = [add("round", k, [state["sum", k]])]
            return
        far_sum = add("add_far", k, state["sum", k])
        state["sum", k] = [far_sum, lax.ppermute(far_sum, "dp", line([(1, 0), (2, 3)]))]

    anywhere = pl.BlockSpec(memory_space=pl.ANY)
    weight_shape = shape((3, 9, channels, outputs), F32)

    def choose(k, last=False):
        ins = state["sum", k]
        place, outs, scratch, specs, out_specs, aliases = None, packed(k), [], None, None, None
        if not last:
            place, outs = k, packed(k) + [weight_shape]
            scratch = [vm((9, half, outputs), F32), pltpu.SemaphoreType.DMA((3,))]
            out_specs = [whole, anywhere]
            if "weight_grad" in state:
                ins = ins + [state["weight_grad"]]
                specs = [whole] * (len(ins) - 1) + [anywhere]
                aliases = {len(ins) - 1: 1}
        got = run(
            functools.partial(choose_kernel, 1.0 / dp, place, dp == 8),
            ins,
            outs,
            scratch,
            f"choose_{k}",
            in_specs=specs,
            out_specs=out_specs,
            aliases=aliases,
        )
        if not last:
            state["weight_grad"] = got[1]
        state["own", k] = got[0]
        state["sum", k] = lax.ppermute(got[0], "dp", cores)

    def weight_out(name, halves, with_bias=False, last=False):
        ins = [state["own" if own else "sum", k] for k, own in halves]
        halves = [(k, own, near[k]) for k, own in halves]
        n = len(ins)
        extra = [state["own", k] for k in range(3)] if with_bias else []
        outs = [weight_shape] + ([shape((3, outputs), F32)] if with_bias else [])

        def kernel(*refs):
            if with_bias:
                bias_kernel(1.0 / dp, body, refs[n : n + 3], refs[-3])
                refs = (*refs[: -3], *refs[-2:])
            weight_out_kernel(1.0 / dp, halves, *refs[:n], refs[-3], *refs[-2:])

        got = run(
            kernel,
            ins + extra + [state["weight_grad"]],
            outs,
            [vm((n, 9, half, outputs), F32), pltpu.SemaphoreType.DMA((n, 7))],
            name,
            in_specs=[whole] * (n + len(extra)) + [anywhere],
            out_specs=[anywhere] + [whole] * (len(outs) - 1),
            aliases={n + len(extra): 0},
            last=last,
        )
        state["weight_grad"] = got[0]
        return got[-1]

    def input_part():
        state["back"] = run(
            functools.partial(input_kernel, (columns, stride), parts),
            [weights] + [state["stack", k] for k in range(3)],
            [shape((total, channels), F32)],
            [vm(weights.shape, BF), pltpu.SemaphoreType.DMA],
            "input_grad",
            in_specs=[far] + [whole] * 3,
        )

    two_levels = False

    def send_back():
        counts = [1, 1, 2] if two_levels else [1] * parts
        outs = [shape((n * size, channels), BF) for n in counts]
        back = run(functools.partial(split_rows_kernel, parts), state["back"], outs, [], "split_rows")
        if two_levels:
            state["back"] = [back[0], back[1], exchange(back[2], 0, parts, dp)]
        else:
            state["back"] = [back[0]] + [swap(back[b], b) for b in range(1, parts)]

    def pass_back():
        own, second, got = state["back"]
        outs = [shape((2 * size, channels), BF)]
        on = run(pass_on_kernel, [second, got], outs, [], "pass_on")[0]
        state["back"] = [own, got, exchange(on, 1, parts, dp)]

    def join_back():
        state["input_grad"] = run(
            functools.partial(join_kernel, (rows, columns, stride), parts),
            state["back"],
            [shape(features.shape, BF)],
            [vm((size, channels_all), F32)],
            "join_channels",
        )[0]

    def merge():
        acts = [state["act", k] for k in range(3)]
        state["active"] = run(
            merge_kernel, acts, [shape(grad_out.shape, BF)], [], "merge_branches"
        )[0]

    k0, k1, k2 = 1, 0, 2
    run(touch_kernel, [weights], [], [], "touch_weights", in_specs=[far])
    if top == 2:
        forward(k0, with_feat=True)
        forward(k1)
        reduce_step(k0, 1)
        forward(k2)
        reduce_step(k1, 1)
        activate(k0)
        reduce_step(k2, 1)
        activate(k1)
        gather_step(k0, 0)
        activate(k2)
        gather_step(k1, 0)
        weight_part(k0)
        gather_step(k2, 0)
        add_cores(k0)
        weight_part(k1)
        weight_part(k2)
        add_cores(k1)
        add_cores(k2)
        add_near(k0)
        input_part()
        send_back()
        add_near(k1)
        add_far(k0)
        add_near(k2)
        add_far(k1)
        choose(k0)
        add_far(k2)
        merge()
        join_back()
        choose(k1)
        choose(k2, last=True)
        weight_out("weight_out_a", [(k0, False), (k1, False)])
        bias_grad = weight_out("weight_out_b", [(k2, True)], with_bias=True)
        weight_out("weight_out_c", [(k2, False)], last=True)
    else:
        forward(k0, with_feat=True)
        forward(k1)
        forward(k2)
        for k in (k0, k1, k2):
            for level in range(1, top):
                reduce_step(k, level)
            activate(k)
            for level in range(top - 2, -1, -1):
                gather_step(k, level)
            weight_part(k)
            add_cores(k)
            add_near(k)
        input_part()
        send_back()
        add_far(k0)
        add_far(k1)
        choose(k0)
        add_far(k2)
        join_back()
        merge()
        choose(k1)
        choose(k2, last=True)
        weight_out("weight_out_a", [(k0, False), (k1, False)])
        bias_grad = weight_out("weight_out_b", [(k2, True)], with_bias=True)
        weight_out("weight_out_c", [(k2, False)], last=True)
    return state["active"], state["input_grad"], state["weight_grad"], bias_grad


def solution(mesh):
    placed = (
        P("dp", "space", None, None),
        P(None, None, "space", None),
        P(),
        P("dp", "space", None, None),
    )
    return jax.shard_map(
        per_device,
        mesh=mesh,
        in_specs=placed,
        out_specs=(
            P("dp", "space", None, None),
            P("dp", "space", None, None),
            P(None, None, "space", None),
            P(),
        ),
        check_vma=False,
    )
```

```python
import functools

import jax
import jax.numpy as jnp
from jax import lax
from jax.experimental import pallas as pl
from jax.experimental.pallas import tpu as pltpu
from jax.sharding import PartitionSpec as P

dilations = (12, 24, 36)
BF = jnp.bfloat16
F32 = jnp.float32
EXTRA = 16


def stride_of(columns):
    return -(-columns // 8) * 8


COSTS = {"input_grad": 0.05, "add_near_0": 0.05, "add_near_2": 1, "add_near_1": 1, "split_rows": 0.05, "add_far_0": 0.05, "add_far_2": 0.05, "add_far_1": 0.05, "merge_branches": 0.05, "join_channels": 0.05, "choose_0": 0.05, "choose_2": 0.05, "choose_1": 0.05, "weight_out_a": 0.05, "weight_out_b": 0.05, "add_cores_1": 1, "join_2": 3, "add_cores_0": 0, "add_cores_2": 0, "weight_grad_2": 0, "pass_on": 0.05, "weight_out_c": 0.05}
UNIT = 1_150_000_000


def call(
    chain, kernel, ins, outs, scratch, name, in_specs=None, out_specs=None, aliases=None, last=False
):
    after = chain[-1:]
    vmem = pl.BlockSpec(memory_space=pltpu.VMEM)
    specs = list(in_specs or [vmem] * len(ins)) + [pl.BlockSpec(memory_space=pl.ANY)] * len(after)
    n, m, k = len(ins), len(after), len(outs)

    def body(*refs):
        rest = refs[n + m + k :]
        if not last:
            rest[0][...] = jnp.zeros(rest[0].shape, F32)
            rest = rest[1:]
        kernel(*refs[:n], *refs[n + m : n + m + k], *rest)

    got = pl.pallas_call(
        body,
        grid=(1,),
        out_shape=(*outs, *([] if last else [shape((8, 128), F32)])),
        in_specs=specs,
        out_specs=(*(out_specs or [vmem] * k), *([] if last else [vmem])),
        scratch_shapes=scratch,
        name=name,
        input_output_aliases=aliases or {},
        compiler_params=pltpu.CompilerParams(vmem_limit_bytes=40 * 1024 * 1024),
        cost_estimate=pl.CostEstimate(
            flops=int(COSTS.get(name, 1.0) * UNIT), bytes_accessed=1024, transcendentals=0
        ),
    )(*ins, *after)
    if last:
        return list(got)
    chain.append(got[-1])
    return list(got[:-1])


def shape(dims, kind):
    return jax.ShapeDtypeStruct(dims, kind)


def flatten_rows(src, scr, rows, columns, stride):
    for r in range(rows):
        scr[stride * r : stride * r + columns] = src[0, r].astype(F32)
        if stride > columns:
            scr[stride * r + columns : stride * (r + 1)] = jnp.zeros(
                (stride - columns, scr.shape[1]), F32
            )


def levels(parts):
    return parts.bit_length() - 1


def flip_bit(core, level, parts):
    return 1 << ((level + core) % levels(parts))


def owner(q, parts):
    core = lax.axis_index("dp") % 2
    at = lax.axis_index("space")
    for level in range(levels(parts)):
        if (q >> (levels(parts) - 1 - level)) & 1:
            at = at ^ jnp.where(core == 0, flip_bit(0, level, parts), flip_bit(1, level, parts))
    return at


def exchange(x, level, parts, dp):
    pairs = []
    for d in range(dp):
        for p in range(parts):
            pairs.append((d * parts + p, d * parts + (p ^ flip_bit(d % 2, level, parts))))
    return lax.ppermute(x, ("dp", "space"), pairs)


def split_kernel(dims, x_ref, *refs):
    rows, columns, stride, parts = dims
    outs, scr = refs[:parts], refs[parts]
    me = lax.axis_index("space")
    flatten_rows(x_ref, scr, rows, columns, stride)
    width = outs[0].shape[1]
    for b in range(parts):
        at = pl.multiple_of((me ^ b) * width, width)
        outs[b][...] = scr[:, pl.ds(at, width)].astype(BF)


def shifted_copies(pad_scr, half_scr, out, columns, stride, shifts):
    total, n = out.shape[0], pad_scr.shape[1]
    pad = (pad_scr.shape[0] - total) // 2
    limit = pad_scr.shape[0] - 8
    half_scr[0:limit] = pad_scr[4 : limit + 4]
    step = 2 * stride
    col = lax.broadcasted_iota(jnp.int32, (step, n), 0)
    col = jnp.where(col >= stride, col - stride, col)

    @pl.loop(0, total // step)
    def _(p):
        base = pl.multiple_of(p * step, step)
        for j, shift in enumerate(shifts):
            off = pad + shift
            if off % 8 == 0:
                v = pad_scr[pl.ds(pl.multiple_of(base + off, 8), step)]
            else:
                v = half_scr[pl.ds(pl.multiple_of(base + off - 4, 8), step)]
            if shift:
                ok = (col + shift >= 0) & (col + shift < columns)
                v = jnp.where(ok, v, 0.0)
            out[pl.ds(base, step), j * n : (j + 1) * n] = v.astype(BF)


def gather_blocks(blocks, pad_scr, pad):
    me = lax.axis_index("space")
    size, n = blocks[0].shape
    total = size * len(blocks)
    pad_scr[0:pad] = jnp.zeros((pad, n), F32)
    pad_scr[pad + total : 2 * pad + total] = jnp.zeros((pad, n), F32)
    for b, block in enumerate(blocks):
        at = pl.multiple_of((me ^ b) * size + pad, 8)
        pad_scr[pl.ds(at, size)] = block[...].astype(F32)


def mm(a, b, ca=1, cb=0):
    return lax.dot_general(a, b, (((ca,), (cb,)), ((), ())), preferred_element_type=F32)


def take_rows(scr, places, size, parts):
    rows = [scr[pl.ds(pl.multiple_of(owner(q, parts) * size, 8), size)] for q in places]
    return jnp.concatenate(rows, axis=0)


def forward_kernel(dims, branch, parts, w_ref, *refs):
    columns, stride = dims
    blocks, outs = refs[:parts], refs[parts:-6]
    pad_scr, half_scr, stack, acc, taps, sem = refs[-6:]
    copy = pltpu.make_async_copy(w_ref.at[branch], taps, sem)
    copy.start()
    spacing = dilations[branch]
    total = acc.shape[0]
    n = blocks[0].shape[1]
    gather_blocks(blocks, pad_scr, stride)
    shifted_copies(pad_scr, half_scr, stack, columns, stride, (-spacing, 0, spacing))
    copy.wait()
    step = spacing * stride
    w = [taps[3 * a : 3 * a + 3].reshape(3 * n, taps.shape[2]) for a in range(3)]
    acc[...] = mm(stack[...], w[1])
    acc[step:] += mm(stack[: total - step], w[0])
    acc[: total - step] += mm(stack[step:], w[2])
    keep, send = outs[:2]
    size = blocks[0].shape[0]
    keep[...] = take_rows(acc, range(parts // 2), size, parts)
    send[...] = take_rows(acc, range(parts // 2, parts), size, parts).astype(BF)
    if len(outs) > 2:
        outs[2][...] = stack[:, n : 2 * n]


def add_half_kernel(kept, got, keep, send):
    x = kept[...] + got[...].astype(F32)
    size = keep.shape[0]
    keep[...] = x[:size]
    send[...] = x[size:].astype(BF)


def join_rows_kernel(a, b, out):
    out[...] = jnp.concatenate([a[...].astype(F32), b[...].astype(F32)], axis=0).astype(BF)


def act_kernel(dims, branch, kept, got, bias_ref, go_ref, act_ref, grad_ref, scr):
    rows, columns, stride = dims
    flatten_rows(go_ref, scr, rows, columns, stride)
    pre = kept[...] + got[...].astype(F32) + bias_ref[branch : branch + 1, :]
    squash = jax.nn.sigmoid(pre)
    slope = squash * (1.0 + pre * (1.0 - squash))
    grad_ref[...] = (scr[...] * slope).astype(BF)
    scr[...] = pre * squash
    for r in range(rows):
        act_ref[0, r] = scr[stride * r : stride * r + columns].astype(BF)


def corner_rows(slab, rows, stride, column):
    return jnp.concatenate([slab[stride * r + column : stride * r + column + 1] for r in range(rows)])


def in_slot(x, slots):
    row = lax.broadcasted_iota(jnp.int32, (slots * x.shape[0], x.shape[1]), 0)
    mine = row // x.shape[0] == lax.axis_index("dp")
    return jnp.where(mine, jnp.concatenate([x] * slots), 0.0)


def weight_kernel(dims, spacing, parts, near, mine, theirs, feat, keep, *refs):
    columns, stride = dims
    send, gstack, gpad, ghalf, full = refs
    core = lax.axis_index("dp") % 2
    total = gstack.shape[0]
    outputs = gpad.shape[1]
    gpad[0:stride] = jnp.zeros((stride, outputs), F32)
    gpad[stride + total :] = jnp.zeros((stride, outputs), F32)
    size = total // parts
    for q in range(parts):
        block = (mine, theirs)[2 * q // parts][...].astype(F32)
        at = q % (parts // 2) * size
        to = pl.multiple_of(owner(q, parts) * size + stride, 8)
        gpad[pl.ds(to, size)] = block[at : at + size]
    shifted_copies(gpad, ghalf, gstack, columns, stride, (spacing, 0, -spacing))
    step = spacing * stride
    at = 0
    for a in range(3):
        if a == 0:
            f, g = feat[: total - step], gstack[step:]
        elif a == 1:
            f, g = feat[...], gstack[...]
        else:
            f, g = feat[step:], gstack[: total - step]
        taps = (1,) if near and a != 1 else (0, 1, 2)
        if len(taps) == 1:
            g = g[:, outputs : 2 * outputs]
        r = mm(f, g, 0, 0)
        for c in range(len(taps)):
            full[at + c] = r[:, c * outputs : (c + 1) * outputs]
        at += len(taps)
    half = full.shape[1] // 2
    body = at * half
    own = full[:at, pl.ds(pl.multiple_of(core * half, half), half)]
    other = full[:at, pl.ds(pl.multiple_of((1 - core) * half, half), half)]
    keep[:body] = own.reshape(body, outputs)
    send[:body] = other.reshape(body, outputs).astype(BF)
    total_bias = jnp.sum(gpad[...], axis=0, keepdims=True)
    row = lax.broadcasted_iota(jnp.int32, (EXTRA, outputs), 0)
    own_bias = jnp.where(row == 0, total_bias, 0.0)
    keep[body : body + EXTRA] = own_bias
    send[body : body + EXTRA] = pack_extra(own_bias)
    if near:
        slots = lax.axis_size("dp")
        ends = (0, total - near * stride)
        last = columns - 1
        fs = [feat[e : e + near * stride].astype(F32) for e in ends]
        gs = [gpad[stride + e : stride + e + near * stride] for e in ends]
        at, n = body + EXTRA, near * slots
        for a in range(2):
            for c in range(2):
                f = in_slot(corner_rows(fs[a], near, stride, c * last), slots)
                g = in_slot(corner_rows(gs[1 - a], near, stride, (1 - c) * last), slots)
                first = core == 0
                keep[at : at + n] = jnp.where(first, f[:, :half], f[:, half:])
                send[at : at + n] = jnp.where(first, f[:, half:], f[:, :half]).astype(BF)
                keep[at + 4 * n : at + 5 * n] = g
                send[at + 4 * n : at + 5 * n] = g.astype(BF)
                at += n


def pack_extra(x):
    total = jnp.sum(x, axis=0, keepdims=True)
    high = total.astype(BF).astype(F32)
    row = lax.broadcasted_iota(jnp.int32, x.shape, 0)
    return jnp.where(row == 0, high, jnp.where(row == 1, total - high, 0.0)).astype(BF)


def add_pack_kernel(body, *refs):
    ins, out_ref = refs[:-1], refs[-1]
    n = ins[0].shape[0]
    for x in ins:
        n = min(n, x.shape[0])
    total = ins[0][:n].astype(F32)
    for x in ins[1:]:
        total = total + x[:n].astype(F32)
    out_ref[:n] = total.astype(BF)
    out_ref[body : body + EXTRA] = pack_extra(total[body : body + EXTRA])
    if out_ref.shape[0] > n:
        out_ref[n:] = jnp.zeros((out_ref.shape[0] - n, out_ref.shape[1]), BF)


def put_half(x, near, out, buf, sems, place, at, scale):
    half, outputs = buf.shape[1:]
    rows = pl.ds(pl.multiple_of(at * half, half), half)
    copies = []

    def send(first, count):
        sem = sems.at[len(copies)]
        src, dst = buf.at[first : first + count], out.at[place, first : first + count, rows]
        copies.append(pltpu.make_async_copy(src, dst, sem))
        copies[-1].start()

    if not near:
        for a in range(3):
            part = x[3 * a * half : 3 * (a + 1) * half].astype(F32) * scale
            buf[3 * a : 3 * a + 3] = part.reshape(3, half, outputs)
            send(3 * a, 3)
        return copies
    i = 0
    for first, count in ((1, 1), (3, 3), (7, 1)):
        part = x[i * half : (i + count) * half].astype(F32) * scale
        buf[first : first + count] = part.reshape(count, half, outputs)
        send(first, count)
        i += count
    n = near * lax.axis_size("dp")
    start = 5 * half + EXTRA
    f, g = x[start : start + 4 * n], x[start + 4 * n : start + 8 * n].astype(F32)
    corner = lax.broadcasted_iota(jnp.int32, g.shape, 0) // n
    spread = jnp.concatenate([jnp.where(corner == i, g, 0.0) for i in range(4)], axis=1)
    r = mm(f, spread.astype(BF), 0, 0) * scale
    for i, t in enumerate((0, 2, 6, 8)):
        buf[t] = r[:, i * outputs : (i + 1) * outputs]
        send(t, 1)
    return copies


def choose_kernel(scale, place, lined, *refs):
    inner = refs[0][...]
    if lined:
        chip = lax.axis_index("dp") // 2
        inner = jnp.where((chip == 1) | (chip == 2), inner, refs[1][...])
    outs = refs[2 if lined else 1 :]
    if place is None:
        outs[0][...] = inner
        return
    own, out, buf, sem = outs[-4:]
    own[...] = inner
    for copy in put_half(inner, 0, out, buf, sem, place, lax.axis_index("dp") % 2, scale):
        copy.wait()


def weight_out_kernel(scale, halves, *refs):
    n = len(halves)
    out, bufs, sems = refs[-3:]
    core = lax.axis_index("dp") % 2
    copies = []
    for i, (place, own, near) in enumerate(halves):
        at = core if own else 1 - core
        copies += put_half(refs[i], near, out, bufs.at[i], sems.at[i], place, at, scale)
    for copy in copies:
        copy.wait()


def bias_kernel(scale, bodies, ins, out, buf, sem):
    for k, x in enumerate(ins):
        body = bodies[k]
        total = jnp.sum(x[body : body + EXTRA].astype(F32), axis=0, keepdims=True)
        buf[k : k + 1, :] = total * scale
    copy = pltpu.make_async_copy(buf, out, sem)
    copy.start()
    return copy


def touch_kernel(w_ref):
    pass


def input_kernel(dims, parts, w_ref, *refs):
    stacks = refs[:3]
    acc, taps, sem = refs[3:]
    copy = pltpu.make_async_copy(w_ref, taps, sem)
    copy.start()
    copy.wait()
    total = acc.shape[0]
    for k, spacing in enumerate(dilations):
        g = stacks[k]
        step = spacing * dims[1]
        for a in (1, 0, 2):
            w = jnp.concatenate([taps[k, 3 * a + c] for c in range(3)], axis=1)
            if a == 1:
                r = mm(g[...], w, 1, 1)
                if k == 0:
                    acc[...] = r
                else:
                    acc[...] += r
            elif a == 0:
                acc[: total - step] += mm(g[step:], w, 1, 1)
            else:
                acc[step:] += mm(g[: total - step], w, 1, 1)


def split_rows_kernel(parts, acc, *outs):
    size = acc.shape[0] // parts
    if len(outs) == 3:
        outs[0][...] = take_rows(acc, [0], size, parts).astype(BF)
        outs[1][...] = take_rows(acc, [1], size, parts).astype(BF)
        outs[2][...] = take_rows(acc, [2, 3], size, parts).astype(BF)
        return
    me = lax.axis_index("space")
    for b in range(parts):
        at = pl.multiple_of((me ^ b) * size, 8)
        outs[b][...] = acc[pl.ds(at, size)].astype(BF)


def pass_on_kernel(own, got, out):
    size = own.shape[0]
    out[:size] = own[...]
    out[size:] = got[size:]


def join_kernel(dims, parts, *refs):
    rows, columns, stride = dims
    blocks, out_ref, scr = refs[:-2], refs[-2], refs[-1]
    me = lax.axis_index("space")
    width, size = blocks[0].shape[1], scr.shape[0]
    if len(blocks) == 3:
        parted = [(blocks[0], 0), (blocks[2], 0), (blocks[1], 0), (blocks[2], 1)]
        places = [owner(q, parts) for q in range(4)]
    else:
        parted = [(block, 0) for block in blocks]
        places = [me ^ b for b in range(parts)]
    for (block, n), place in zip(parted, places):
        at = pl.multiple_of(place * width, width)
        scr[:, pl.ds(at, width)] = block[n * size : (n + 1) * size].astype(F32)
    for r in range(rows):
        out_ref[0, r] = scr[stride * r : stride * r + columns].astype(BF)


def merge_kernel(*refs):
    ins, out = refs[:-1], refs[-1]
    n = ins[0].shape[3]
    for k, x in enumerate(ins):
        out[:, :, :, k * n : (k + 1) * n] = x[...]


def swap(x, bit):
    n = lax.axis_size("space")
    return lax.ppermute(x, "space", [(i, i ^ bit) for i in range(n)])


def per_device(features, weights, bias, grad_out):
    images, rows, columns, channels_all = features.shape
    assert images == 1
    parts = lax.axis_size("space")
    dp = lax.axis_size("dp")
    channels, outputs = weights.shape[2], weights.shape[3]
    stride = stride_of(columns)
    size = rows * stride
    total = size * parts
    padded = total + 2 * stride
    vm = pltpu.VMEM
    whole = pl.BlockSpec(memory_space=pltpu.VMEM)
    far = pl.BlockSpec(memory_space=pltpu.HBM)
    top = levels(parts)
    cores = [(i, i ^ 1) for i in range(dp)]
    half = channels // 2
    near, body, kept_rows = [], [], []
    for spacing in dilations:
        few = rows * parts - spacing
        if dp == 8 and few == 4 and columns - spacing == 1 and half == outputs and size % 16 == 0:
            near.append(few)
            body.append(5 * half)
            kept_rows.append(5 * half + EXTRA + 8 * few * dp)
        else:
            near.append(0)
            body.append(9 * half)
            kept_rows.append(9 * half + EXTRA)

    def packed(k):
        return [shape((kept_rows[k] + 16, outputs), BF)]

    chain = []
    run = functools.partial(call, chain)

    mine = run(
        functools.partial(split_kernel, (rows, columns, stride, parts)),
        [features],
        [shape((size, channels), BF)] * parts,
        [vm((size, channels_all), F32)],
        "split_channels",
    )
    feats = [mine[0]] + [swap(mine[b], b) for b in range(1, parts)]

    state = {}
    rows_kept = size * parts // 2

    def forward(k, with_feat=False):
        outs = [shape((rows_kept, outputs), F32), shape((rows_kept, outputs), BF)]
        if with_feat:
            outs.append(shape((total, channels), BF))
        got = run(
            functools.partial(forward_kernel, (columns, stride), k, parts),
            [weights] + feats,
            outs,
            [
                vm((padded, channels), F32),
                vm((padded, channels), F32),
                vm((total, 3 * channels), BF),
                vm((total, outputs), F32),
                vm((9, channels, outputs), BF),
                pltpu.SemaphoreType.DMA,
            ],
            f"forward_{k}",
            in_specs=[far] + [whole] * parts,
        )
        if with_feat:
            state["feat"] = got[2]
        state[k] = (got[0], exchange(got[1], 0, parts, dp))

    def reduce_step(k, level):
        keep, got = state[k]
        n = keep.shape[0] // 2
        outs = [shape((n, outputs), F32), shape((n, outputs), BF)]
        keep, send = run(add_half_kernel, [keep, got], outs, [], f"add_{k}")
        state[k] = (keep, exchange(send, level, parts, dp))

    def activate(k):
        keep, got = state[k]
        act, grad = run(
            functools.partial(act_kernel, (rows, columns, stride), k),
            [keep, got, bias, grad_out],
            [shape((1, rows, columns, outputs), BF), shape((size, outputs), BF)],
            [vm((size, outputs), F32)],
            f"activation_{k}",
            in_specs=[whole] * 3 + [pl.BlockSpec((1, rows, columns, outputs), lambda i: (0, 0, 0, k))],
        )
        state[k] = (grad, exchange(grad, top - 1, parts, dp))
        state["act", k] = act

    def gather_step(k, level):
        own, got = state[k]
        outs = [shape((2 * own.shape[0], outputs), BF)]
        both = run(join_rows_kernel, [own, got], outs, [], f"join_{k}")[0]
        state[k] = (both, exchange(both, level, parts, dp))

    def weight_part(k):
        own, got = state[k]
        keep, send, stack = run(
            functools.partial(weight_kernel, (columns, stride), dilations[k], parts, near[k]),
            [own, got, state["feat"]],
            [
                shape((kept_rows[k], outputs), F32),
                shape((kept_rows[k], outputs), BF),
                shape((total, 3 * outputs), BF),
            ],
            [
                vm((padded, outputs), F32),
                vm((padded, outputs), F32),
                vm((9, channels, outputs), F32),
            ],
            f"weight_grad_{k}",
        )
        state["stack", k] = stack
        state["sum", k] = [keep, lax.ppermute(send, "dp", cores)]

    def line(pairs):
        return [(2 * a + c, 2 * b + c) for a, b in pairs for c in range(2)]

    def add(name, k, ins):
        kernel = functools.partial(add_pack_kernel, body[k])
        return run(kernel, ins, packed(k), [], f"{name}_{k}")[0]

    def add_cores(k):
        got = state["sum", k]
        if dp != 8:
            kept = got[0] + got[1].astype(F32)
            groups = [[2 * i + c for i in range(dp // 2)] for c in range(2)]
            state["sum", k] = lax.psum(kept, "dp", axis_index_groups=groups)
            return
        near = add("add_cores", k, got)
        state["sum", k] = got + [lax.ppermute(near, "dp", line([(0, 1), (3, 2)]))]

    def add_near(k):
        if dp == 8:
            near = add("add_near", k, state["sum", k])
            state["sum", k] = [near, lax.ppermute(near, "dp", line([(1, 2), (2, 1)]))]

    def add_far(k):
        if dp != 8:
            state["sum", k] = [add("round", k, [state["sum", k]])]
            return
        far_sum = add("add_far", k, state["sum", k])
        state["sum", k] = [far_sum, lax.ppermute(far_sum, "dp", line([(1, 0), (2, 3)]))]

    anywhere = pl.BlockSpec(memory_space=pl.ANY)
    weight_shape = shape((3, 9, channels, outputs), F32)

    def choose(k, last=False):
        ins = state["sum", k]
        place, outs, scratch, specs, out_specs, aliases = None, packed(k), [], None, None, None
        if not last:
            place, outs = k, packed(k) + [weight_shape]
            scratch = [vm((9, half, outputs), F32), pltpu.SemaphoreType.DMA((3,))]
            out_specs = [whole, anywhere]
            if "weight_grad" in state:
                ins = ins + [state["weight_grad"]]
                specs = [whole] * (len(ins) - 1) + [anywhere]
                aliases = {len(ins) - 1: 1}
        got = run(
            functools.partial(choose_kernel, 1.0 / dp, place, dp == 8),
            ins,
            outs,
            scratch,
            f"choose_{k}",
            in_specs=specs,
            out_specs=out_specs,
            aliases=aliases,
        )
        if not last:
            state["weight_grad"] = got[1]
        state["own", k] = got[0]
        state["sum", k] = lax.ppermute(got[0], "dp", cores)

    def weight_out(name, halves, with_bias=False, last=False):
        ins = [state["own" if own else "sum", k] for k, own in halves]
        halves = [(k, own, near[k]) for k, own in halves]
        n = len(ins)
        extra = [state["own", k] for k in range(3)] if with_bias else []
        outs = [weight_shape] + ([shape((3, outputs), F32)] if with_bias else [])

        scratch = [vm((n, 9, half, outputs), F32), pltpu.SemaphoreType.DMA((n, 7))]
        if with_bias:
            scratch += [vm((3, outputs), F32), pltpu.SemaphoreType.DMA]

        def kernel(*refs):
            main = functools.partial(weight_out_kernel, 1.0 / dp, halves, *refs[:n])
            if with_bias:
                out, bias_out, bufs, sems, buf, sem = refs[-6:]
                copy = bias_kernel(1.0 / dp, body, refs[n : n + 3], bias_out, buf, sem)
                main(out, bufs, sems)
                copy.wait()
            else:
                main(*refs[-3:])

        got = run(
            kernel,
            ins + extra + [state["weight_grad"]],
            outs,
            scratch,
            name,
            in_specs=[whole] * (n + len(extra)) + [anywhere],
            out_specs=[anywhere] * len(outs),
            aliases={n + len(extra): 0},
            last=last,
        )
        state["weight_grad"] = got[0]
        return got[-1]

    def input_part():
        state["back"] = run(
            functools.partial(input_kernel, (columns, stride), parts),
            [weights] + [state["stack", k] for k in range(3)],
            [shape((total, channels), F32)],
            [vm(weights.shape, BF), pltpu.SemaphoreType.DMA],
            "input_grad",
            in_specs=[far] + [whole] * 3,
        )

    two_levels = False

    def send_back():
        counts = [1, 1, 2] if two_levels else [1] * parts
        outs = [shape((n * size, channels), BF) for n in counts]
        back = run(functools.partial(split_rows_kernel, parts), state["back"], outs, [], "split_rows")
        if two_levels:
            state["back"] = [back[0], back[1], exchange(back[2], 0, parts, dp)]
        else:
            state["back"] = [back[0]] + [swap(back[b], b) for b in range(1, parts)]

    def pass_back():
        own, second, got = state["back"]
        outs = [shape((2 * size, channels), BF)]
        on = run(pass_on_kernel, [second, got], outs, [], "pass_on")[0]
        state["back"] = [own, got, exchange(on, 1, parts, dp)]

    def join_back():
        state["input_grad"] = run(
            functools.partial(join_kernel, (rows, columns, stride), parts),
            state["back"],
            [shape(features.shape, BF)],
            [vm((size, channels_all), F32)],
            "join_channels",
        )[0]

    def merge():
        acts = [state["act", k] for k in range(3)]
        state["active"] = run(
            merge_kernel, acts, [shape(grad_out.shape, BF)], [], "merge_branches"
        )[0]

    k0, k1, k2 = 1, 0, 2
    run(touch_kernel, [weights], [], [], "touch_weights", in_specs=[far])
    if top == 2:
        forward(k0, with_feat=True)
        forward(k1)
        reduce_step(k0, 1)
        forward(k2)
        reduce_step(k1, 1)
        activate(k0)
        reduce_step(k2, 1)
        activate(k1)
        gather_step(k0, 0)
        activate(k2)
        gather_step(k1, 0)
        weight_part(k0)
        gather_step(k2, 0)
        add_cores(k0)
        weight_part(k1)
        weight_part(k2)
        add_cores(k1)
        add_cores(k2)
        add_near(k0)
        input_part()
        send_back()
        add_near(k1)
        add_far(k0)
        add_near(k2)
        add_far(k1)
        choose(k0)
        add_far(k2)
        merge()
        join_back()
        choose(k1)
        choose(k2, last=True)
        weight_out("weight_out_a", [(k0, False), (k1, False)])
        bias_grad = weight_out("weight_out_b", [(k2, True)], with_bias=True)
        weight_out("weight_out_c", [(k2, False)], last=True)
    else:
        forward(k0, with_feat=True)
        forward(k1)
        forward(k2)
        for k in (k0, k1, k2):
            for level in range(1, top):
                reduce_step(k, level)
            activate(k)
            for level in range(top - 2, -1, -1):
                gather_step(k, level)
            weight_part(k)
            add_cores(k)
            add_near(k)
        input_part()
        send_back()
        add_far(k0)
        add_far(k1)
        choose(k0)
        add_far(k2)
        join_back()
        merge()
        choose(k1)
        choose(k2, last=True)
        weight_out("weight_out_a", [(k0, False), (k1, False)])
        bias_grad = weight_out("weight_out_b", [(k2, True)], with_bias=True)
        weight_out("weight_out_c", [(k2, False)], last=True)
    return state["active"], state["input_grad"], state["weight_grad"], bias_grad


def solution(mesh):
    placed = (
        P("dp", "space", None, None),
        P(None, None, "space", None),
        P(),
        P("dp", "space", None, None),
    )
    return jax.shard_map(
        per_device,
        mesh=mesh,
        in_specs=placed,
        out_specs=(
            P("dp", "space", None, None),
            P("dp", "space", None, None),
            P(None, None, "space", None),
            P(),
        ),
        check_vma=False,
    )
```

```python
import functools

import jax
import jax.numpy as jnp
from jax import lax
from jax.experimental import pallas as pl
from jax.experimental.pallas import tpu as pltpu
from jax.sharding import PartitionSpec as P

dilations = (12, 24, 36)
BF = jnp.bfloat16
F32 = jnp.float32
EXTRA = 16


def stride_of(columns):
    return -(-columns // 8) * 8


COSTS = {"input_grad": 0.05, "add_near_0": 0.05, "add_near_2": 1, "add_near_1": 1, "split_rows": 0.05, "add_far_0": 0.05, "add_far_2": 0.05, "add_far_1": 0.05, "merge_branches": 0.05, "join_channels": 0.05, "choose_0": 0.05, "choose_2": 0.05, "choose_1": 0.05, "weight_out_a": 0.05, "weight_out_b": 0.05, "add_cores_1": 1, "join_2": 3, "add_cores_0": 0, "add_cores_2": 0, "weight_grad_2": 0, "pass_on": 0.05, "weight_out_c": 0.05}
UNIT = 1_150_000_000


def call(
    chain, kernel, ins, outs, scratch, name, in_specs=None, out_specs=None, aliases=None, last=False
):
    after = chain[-1:]
    vmem = pl.BlockSpec(memory_space=pltpu.VMEM)
    specs = list(in_specs or [vmem] * len(ins)) + [pl.BlockSpec(memory_space=pl.ANY)] * len(after)
    n, m, k = len(ins), len(after), len(outs)

    def body(*refs):
        rest = refs[n + m + k :]
        if not last:
            rest[0][...] = jnp.zeros(rest[0].shape, F32)
            rest = rest[1:]
        kernel(*refs[:n], *refs[n + m : n + m + k], *rest)

    got = pl.pallas_call(
        body,
        grid=(1,),
        out_shape=(*outs, *([] if last else [shape((8, 128), F32)])),
        in_specs=specs,
        out_specs=(*(out_specs or [vmem] * k), *([] if last else [vmem])),
        scratch_shapes=scratch,
        name=name,
        input_output_aliases=aliases or {},
        compiler_params=pltpu.CompilerParams(vmem_limit_bytes=40 * 1024 * 1024),
        cost_estimate=pl.CostEstimate(
            flops=int(COSTS.get(name, 1.0) * UNIT), bytes_accessed=1024, transcendentals=0
        ),
    )(*ins, *after)
    if last:
        return list(got)
    chain.append(got[-1])
    return list(got[:-1])


def shape(dims, kind):
    return jax.ShapeDtypeStruct(dims, kind)


def flatten_rows(src, scr, rows, columns, stride):
    for r in range(rows):
        scr[stride * r : stride * r + columns] = src[0, r].astype(F32)
        if stride > columns:
            scr[stride * r + columns : stride * (r + 1)] = jnp.zeros(
                (stride - columns, scr.shape[1]), F32
            )


def levels(parts):
    return parts.bit_length() - 1


def flip_bit(core, level, parts):
    return 1 << ((level + core) % levels(parts))


def owner(q, parts):
    core = lax.axis_index("dp") % 2
    at = lax.axis_index("space")
    for level in range(levels(parts)):
        if (q >> (levels(parts) - 1 - level)) & 1:
            at = at ^ jnp.where(core == 0, flip_bit(0, level, parts), flip_bit(1, level, parts))
    return at


def exchange(x, level, parts, dp):
    pairs = []
    for d in range(dp):
        for p in range(parts):
            pairs.append((d * parts + p, d * parts + (p ^ flip_bit(d % 2, level, parts))))
    return lax.ppermute(x, ("dp", "space"), pairs)


def split_kernel(dims, x_ref, *refs):
    rows, columns, stride, parts = dims
    outs, scr = refs[:parts], refs[parts]
    me = lax.axis_index("space")
    flatten_rows(x_ref, scr, rows, columns, stride)
    width = outs[0].shape[1]
    for b in range(parts):
        at = pl.multiple_of((me ^ b) * width, width)
        outs[b][...] = scr[:, pl.ds(at, width)].astype(BF)


def shifted_copies(pad_scr, half_scr, out, columns, stride, shifts):
    total, n = out.shape[0], pad_scr.shape[1]
    pad = (pad_scr.shape[0] - total) // 2
    limit = pad_scr.shape[0] - 8
    half_scr[0:limit] = pad_scr[4 : limit + 4]
    step = 2 * stride
    col = lax.broadcasted_iota(jnp.int32, (step, n), 0)
    col = jnp.where(col >= stride, col - stride, col)

    @pl.loop(0, total // step)
    def _(p):
        base = pl.multiple_of(p * step, step)
        for j, shift in enumerate(shifts):
            off = pad + shift
            if off % 8 == 0:
                v = pad_scr[pl.ds(pl.multiple_of(base + off, 8), step)]
            else:
                v = half_scr[pl.ds(pl.multiple_of(base + off - 4, 8), step)]
            if shift:
                ok = (col + shift >= 0) & (col + shift < columns)
                v = jnp.where(ok, v, 0.0)
            out[pl.ds(base, step), j * n : (j + 1) * n] = v.astype(BF)


def gather_blocks(blocks, pad_scr, pad):
    me = lax.axis_index("space")
    size, n = blocks[0].shape
    total = size * len(blocks)
    pad_scr[0:pad] = jnp.zeros((pad, n), F32)
    pad_scr[pad + total : 2 * pad + total] = jnp.zeros((pad, n), F32)
    for b, block in enumerate(blocks):
        at = pl.multiple_of((me ^ b) * size + pad, 8)
        pad_scr[pl.ds(at, size)] = block[...].astype(F32)


def mm(a, b, ca=1, cb=0):
    return lax.dot_general(a, b, (((ca,), (cb,)), ((), ())), preferred_element_type=F32)


def take_rows(scr, places, size, parts):
    rows = [scr[pl.ds(pl.multiple_of(owner(q, parts) * size, 8), size)] for q in places]
    return jnp.concatenate(rows, axis=0)


def forward_kernel(dims, branch, parts, w_ref, *refs):
    columns, stride = dims
    blocks, outs = refs[:parts], refs[parts:-6]
    pad_scr, half_scr, stack, acc, taps, sem = refs[-6:]
    copy = pltpu.make_async_copy(w_ref.at[branch], taps, sem)
    copy.start()
    spacing = dilations[branch]
    total = acc.shape[0]
    n = blocks[0].shape[1]
    gather_blocks(blocks, pad_scr, stride)
    shifted_copies(pad_scr, half_scr, stack, columns, stride, (-spacing, 0, spacing))
    copy.wait()
    step = spacing * stride
    w = [taps[3 * a : 3 * a + 3].reshape(3 * n, taps.shape[2]) for a in range(3)]
    acc[...] = mm(stack[...], w[1])
    acc[step:] += mm(stack[: total - step], w[0])
    acc[: total - step] += mm(stack[step:], w[2])
    keep, send = outs[:2]
    size = blocks[0].shape[0]
    keep[...] = take_rows(acc, range(parts // 2), size, parts)
    send[...] = take_rows(acc, range(parts // 2, parts), size, parts).astype(BF)
    if len(outs) > 2:
        outs[2][...] = stack[:, n : 2 * n]


def add_half_kernel(kept, got, keep, send):
    x = kept[...] + got[...].astype(F32)
    size = keep.shape[0]
    keep[...] = x[:size]
    send[...] = x[size:].astype(BF)


def join_rows_kernel(a, b, out):
    out[...] = jnp.concatenate([a[...].astype(F32), b[...].astype(F32)], axis=0).astype(BF)


def act_kernel(dims, branch, kept, got, bias_ref, go_ref, act_ref, grad_ref, scr):
    rows, columns, stride = dims
    flatten_rows(go_ref, scr, rows, columns, stride)
    pre = kept[...] + got[...].astype(F32) + bias_ref[branch : branch + 1, :]
    squash = jax.nn.sigmoid(pre)
    slope = squash * (1.0 + pre * (1.0 - squash))
    grad_ref[...] = (scr[...] * slope).astype(BF)
    scr[...] = pre * squash
    for r in range(rows):
        act_ref[0, r] = scr[stride * r : stride * r + columns].astype(BF)


def corner_rows(slab, rows, stride, column):
    return jnp.concatenate([slab[stride * r + column : stride * r + column + 1] for r in range(rows)])


def in_slot(x, slots):
    row = lax.broadcasted_iota(jnp.int32, (slots * x.shape[0], x.shape[1]), 0)
    mine = row // x.shape[0] == lax.axis_index("dp")
    return jnp.where(mine, jnp.concatenate([x] * slots), 0.0)


def weight_kernel(dims, spacing, parts, near, mine, theirs, feat, keep, *refs):
    columns, stride = dims
    send, gstack, gpad, ghalf, full = refs
    core = lax.axis_index("dp") % 2
    total = gstack.shape[0]
    outputs = gpad.shape[1]
    gpad[0:stride] = jnp.zeros((stride, outputs), F32)
    gpad[stride + total :] = jnp.zeros((stride, outputs), F32)
    size = total // parts
    for q in range(parts):
        block = (mine, theirs)[2 * q // parts][...].astype(F32)
        at = q % (parts // 2) * size
        to = pl.multiple_of(owner(q, parts) * size + stride, 8)
        gpad[pl.ds(to, size)] = block[at : at + size]
    shifted_copies(gpad, ghalf, gstack, columns, stride, (spacing, 0, -spacing))
    step = spacing * stride
    at = 0
    for a in range(3):
        if a == 0:
            f, g = feat[: total - step], gstack[step:]
        elif a == 1:
            f, g = feat[...], gstack[...]
        else:
            f, g = feat[step:], gstack[: total - step]
        taps = (1,) if near and a != 1 else (0, 1, 2)
        if len(taps) == 1:
            g = g[:, outputs : 2 * outputs]
        r = mm(f, g, 0, 0)
        for c in range(len(taps)):
            full[at + c] = r[:, c * outputs : (c + 1) * outputs]
        at += len(taps)
    half = full.shape[1] // 2
    body = at * half
    own = full[:at, pl.ds(pl.multiple_of(core * half, half), half)]
    other = full[:at, pl.ds(pl.multiple_of((1 - core) * half, half), half)]
    keep[:body] = own.reshape(body, outputs)
    send[:body] = other.reshape(body, outputs).astype(BF)
    total_bias = jnp.sum(gpad[...], axis=0, keepdims=True)
    row = lax.broadcasted_iota(jnp.int32, (EXTRA, outputs), 0)
    own_bias = jnp.where(row == 0, total_bias, 0.0)
    keep[body : body + EXTRA] = own_bias
    send[body : body + EXTRA] = pack_extra(own_bias)
    if near:
        slots = lax.axis_size("dp")
        ends = (0, total - near * stride)
        last = columns - 1
        fs = [feat[e : e + near * stride].astype(F32) for e in ends]
        gs = [gpad[stride + e : stride + e + near * stride] for e in ends]
        at, n = body + EXTRA, near * slots
        for a in range(2):
            for c in range(2):
                f = in_slot(corner_rows(fs[a], near, stride, c * last), slots)
                g = in_slot(corner_rows(gs[1 - a], near, stride, (1 - c) * last), slots)
                first = core == 0
                keep[at : at + n] = jnp.where(first, f[:, :half], f[:, half:])
                send[at : at + n] = jnp.where(first, f[:, half:], f[:, :half]).astype(BF)
                keep[at + 4 * n : at + 5 * n] = g
                send[at + 4 * n : at + 5 * n] = g.astype(BF)
                at += n


def pack_extra(x):
    total = jnp.sum(x, axis=0, keepdims=True)
    high = total.astype(BF).astype(F32)
    row = lax.broadcasted_iota(jnp.int32, x.shape, 0)
    return jnp.where(row == 0, high, jnp.where(row == 1, total - high, 0.0)).astype(BF)


def add_pack_kernel(body, *refs):
    ins, out_ref = refs[:-1], refs[-1]
    n = ins[0].shape[0]
    for x in ins:
        n = min(n, x.shape[0])
    total = ins[0][:n].astype(F32)
    for x in ins[1:]:
        total = total + x[:n].astype(F32)
    out_ref[:n] = total.astype(BF)
    out_ref[body : body + EXTRA] = pack_extra(total[body : body + EXTRA])
    if out_ref.shape[0] > n:
        out_ref[n:] = jnp.zeros((out_ref.shape[0] - n, out_ref.shape[1]), BF)


def put_half(x, near, out, buf, sems, place, at, scale):
    half, outputs = buf.shape[1:]
    rows = pl.ds(pl.multiple_of(at * half, half), half)
    copies = []

    def send(first, count):
        sem = sems.at[len(copies)]
        src, dst = buf.at[first : first + count], out.at[place, first : first + count, rows]
        copies.append(pltpu.make_async_copy(src, dst, sem))
        copies[-1].start()

    if not near:
        for a in range(3):
            part = x[3 * a * half : 3 * (a + 1) * half].astype(F32) * scale
            buf[3 * a : 3 * a + 3] = part.reshape(3, half, outputs)
            send(3 * a, 3)
        return copies
    i = 0
    for first, count in ((1, 1), (3, 3), (7, 1)):
        part = x[i * half : (i + count) * half].astype(F32) * scale
        buf[first : first + count] = part.reshape(count, half, outputs)
        send(first, count)
        i += count
    n = near * lax.axis_size("dp")
    start = 5 * half + EXTRA
    f, g = x[start : start + 4 * n], x[start + 4 * n : start + 8 * n].astype(F32)
    corner = lax.broadcasted_iota(jnp.int32, g.shape, 0) // n
    spread = jnp.concatenate([jnp.where(corner == i, g, 0.0) for i in range(4)], axis=1)
    r = mm(f, spread.astype(BF), 0, 0) * scale
    for i, t in enumerate((0, 2, 6, 8)):
        buf[t] = r[:, i * outputs : (i + 1) * outputs]
        send(t, 1)
    return copies


def choose_kernel(scale, place, lined, *refs):
    inner = refs[0][...]
    if lined:
        chip = lax.axis_index("dp") // 2
        inner = jnp.where((chip == 1) | (chip == 2), inner, refs[1][...])
    outs = refs[2 if lined else 1 :]
    if place is None:
        outs[0][...] = inner
        return
    own, out, buf, sem = outs[-4:]
    own[...] = inner
    for copy in put_half(inner, 0, out, buf, sem, place, lax.axis_index("dp") % 2, scale):
        copy.wait()


def weight_out_kernel(scale, halves, *refs):
    n = len(halves)
    out, bufs, sems = refs[-3:]
    core = lax.axis_index("dp") % 2
    copies = []
    for i, (place, own, near) in enumerate(halves):
        at = core if own else 1 - core
        copies += put_half(refs[i], near, out, bufs.at[i], sems.at[i], place, at, scale)
    for copy in copies:
        copy.wait()


def bias_kernel(scale, bodies, ins, out, buf, sem):
    for k, x in enumerate(ins):
        body = bodies[k]
        total = jnp.sum(x[body : body + EXTRA].astype(F32), axis=0, keepdims=True)
        buf[k : k + 1, :] = total * scale
    copy = pltpu.make_async_copy(buf, out, sem)
    copy.start()
    return copy


def touch_kernel(w_ref):
    pass


def input_kernel(dims, parts, w_ref, *refs):
    stacks = refs[:3]
    acc, taps, sem = refs[3:]
    copy = pltpu.make_async_copy(w_ref, taps, sem)
    copy.start()
    copy.wait()
    total = acc.shape[0]
    for k, spacing in enumerate(dilations):
        g = stacks[k]
        step = spacing * dims[1]
        for a in (1, 0, 2):
            w = jnp.concatenate([taps[k, 3 * a + c] for c in range(3)], axis=1)
            if a == 1:
                r = mm(g[...], w, 1, 1)
                if k == 0:
                    acc[...] = r
                else:
                    acc[...] += r
            elif a == 0:
                acc[: total - step] += mm(g[step:], w, 1, 1)
            else:
                acc[step:] += mm(g[: total - step], w, 1, 1)


def split_rows_kernel(parts, acc, *outs):
    size = acc.shape[0] // parts
    if len(outs) == 3:
        outs[0][...] = take_rows(acc, [0], size, parts).astype(BF)
        outs[1][...] = take_rows(acc, [1], size, parts).astype(BF)
        outs[2][...] = take_rows(acc, [2, 3], size, parts).astype(BF)
        return
    me = lax.axis_index("space")
    for b in range(parts):
        at = pl.multiple_of((me ^ b) * size, 8)
        outs[b][...] = acc[pl.ds(at, size)].astype(BF)


def pass_on_kernel(own, got, out):
    size = own.shape[0]
    out[:size] = own[...]
    out[size:] = got[size:]


def join_kernel(dims, parts, *refs):
    rows, columns, stride = dims
    blocks, out_ref, scr = refs[:-2], refs[-2], refs[-1]
    me = lax.axis_index("space")
    width, size = blocks[0].shape[1], scr.shape[0]
    if len(blocks) == 3:
        parted = [(blocks[0], 0), (blocks[2], 0), (blocks[1], 0), (blocks[2], 1)]
        places = [owner(q, parts) for q in range(4)]
    else:
        parted = [(block, 0) for block in blocks]
        places = [me ^ b for b in range(parts)]
    for (block, n), place in zip(parted, places):
        at = pl.multiple_of(place * width, width)
        scr[:, pl.ds(at, width)] = block[n * size : (n + 1) * size].astype(F32)
    for r in range(rows):
        out_ref[0, r] = scr[stride * r : stride * r + columns].astype(BF)


def merge_kernel(*refs):
    ins, out = refs[:-1], refs[-1]
    n = ins[0].shape[3]
    for k, x in enumerate(ins):
        out[:, :, :, k * n : (k + 1) * n] = x[...]


def swap(x, bit):
    n = lax.axis_size("space")
    return lax.ppermute(x, "space", [(i, i ^ bit) for i in range(n)])


def per_device(features, weights, bias, grad_out):
    images, rows, columns, channels_all = features.shape
    assert images == 1
    parts = lax.axis_size("space")
    dp = lax.axis_size("dp")
    channels, outputs = weights.shape[2], weights.shape[3]
    stride = stride_of(columns)
    size = rows * stride
    total = size * parts
    padded = total + 2 * stride
    vm = pltpu.VMEM
    whole = pl.BlockSpec(memory_space=pltpu.VMEM)
    far = pl.BlockSpec(memory_space=pltpu.HBM)
    top = levels(parts)
    cores = [(i, i ^ 1) for i in range(dp)]
    half = channels // 2
    near, body, kept_rows = [], [], []
    for spacing in dilations:
        few = rows * parts - spacing
        if dp == 8 and few == 4 and columns - spacing == 1 and half == outputs and size % 16 == 0:
            near.append(few)
            body.append(5 * half)
            kept_rows.append(5 * half + EXTRA + 8 * few * dp)
        else:
            near.append(0)
            body.append(9 * half)
            kept_rows.append(9 * half + EXTRA)

    def packed(k):
        return [shape((kept_rows[k] + (0 if near[k] else 16), outputs), BF)]

    chain = []
    run = functools.partial(call, chain)

    mine = run(
        functools.partial(split_kernel, (rows, columns, stride, parts)),
        [features],
        [shape((size, channels), BF)] * parts,
        [vm((size, channels_all), F32)],
        "split_channels",
    )
    feats = [mine[0]] + [swap(mine[b], b) for b in range(1, parts)]

    state = {}
    rows_kept = size * parts // 2

    def forward(k, with_feat=False):
        outs = [shape((rows_kept, outputs), F32), shape((rows_kept, outputs), BF)]
        if with_feat:
            outs.append(shape((total, channels), BF))
        got = run(
            functools.partial(forward_kernel, (columns, stride), k, parts),
            [weights] + feats,
            outs,
            [
                vm((padded, channels), F32),
                vm((padded, channels), F32),
                vm((total, 3 * channels), BF),
                vm((total, outputs), F32),
                vm((9, channels, outputs), BF),
                pltpu.SemaphoreType.DMA,
            ],
            f"forward_{k}",
            in_specs=[far] + [whole] * parts,
        )
        if with_feat:
            state["feat"] = got[2]
        state[k] = (got[0], exchange(got[1], 0, parts, dp))

    def reduce_step(k, level):
        keep, got = state[k]
        n = keep.shape[0] // 2
        outs = [shape((n, outputs), F32), shape((n, outputs), BF)]
        keep, send = run(add_half_kernel, [keep, got], outs, [], f"add_{k}")
        state[k] = (keep, exchange(send, level, parts, dp))

    def activate(k):
        keep, got = state[k]
        act, grad = run(
            functools.partial(act_kernel, (rows, columns, stride), k),
            [keep, got, bias, grad_out],
            [shape((1, rows, columns, outputs), BF), shape((size, outputs), BF)],
            [vm((size, outputs), F32)],
            f"activation_{k}",
            in_specs=[whole] * 3 + [pl.BlockSpec((1, rows, columns, outputs), lambda i: (0, 0, 0, k))],
        )
        state[k] = (grad, exchange(grad, top - 1, parts, dp))
        state["act", k] = act

    def gather_step(k, level):
        own, got = state[k]
        outs = [shape((2 * own.shape[0], outputs), BF)]
        both = run(join_rows_kernel, [own, got], outs, [], f"join_{k}")[0]
        state[k] = (both, exchange(both, level, parts, dp))

    def weight_part(k):
        own, got = state[k]
        keep, send, stack = run(
            functools.partial(weight_kernel, (columns, stride), dilations[k], parts, near[k]),
            [own, got, state["feat"]],
            [
                shape((kept_rows[k], outputs), F32),
                shape((kept_rows[k], outputs), BF),
                shape((total, 3 * outputs), BF),
            ],
            [
                vm((padded, outputs), F32),
                vm((padded, outputs), F32),
                vm((9, channels, outputs), F32),
            ],
            f"weight_grad_{k}",
        )
        state["stack", k] = stack
        state["sum", k] = [keep, lax.ppermute(send, "dp", cores)]

    def line(pairs):
        return [(2 * a + c, 2 * b + c) for a, b in pairs for c in range(2)]

    def add(name, k, ins):
        kernel = functools.partial(add_pack_kernel, body[k])
        return run(kernel, ins, packed(k), [], f"{name}_{k}")[0]

    def add_cores(k):
        got = state["sum", k]
        if dp != 8:
            kept = got[0] + got[1].astype(F32)
            groups = [[2 * i + c for i in range(dp // 2)] for c in range(2)]
            state["sum", k] = lax.psum(kept, "dp", axis_index_groups=groups)
            return
        near = add("add_cores", k, got)
        state["sum", k] = got + [lax.ppermute(near, "dp", line([(0, 1), (3, 2)]))]

    def add_near(k):
        if dp == 8:
            near = add("add_near", k, state["sum", k])
            state["sum", k] = [near, lax.ppermute(near, "dp", line([(1, 2), (2, 1)]))]

    def add_far(k):
        if dp != 8:
            state["sum", k] = [add("round", k, [state["sum", k]])]
            return
        far_sum = add("add_far", k, state["sum", k])
        state["sum", k] = [far_sum, lax.ppermute(far_sum, "dp", line([(1, 0), (2, 3)]))]

    anywhere = pl.BlockSpec(memory_space=pl.ANY)
    weight_shape = shape((3, 9, channels, outputs), F32)

    def choose(k, last=False):
        ins = state["sum", k]
        place, outs, scratch, specs, out_specs, aliases = None, packed(k), [], None, None, None
        if not last:
            place, outs = k, packed(k) + [weight_shape]
            scratch = [vm((9, half, outputs), F32), pltpu.SemaphoreType.DMA((3,))]
            out_specs = [whole, anywhere]
            if "weight_grad" in state:
                ins = ins + [state["weight_grad"]]
                specs = [whole] * (len(ins) - 1) + [anywhere]
                aliases = {len(ins) - 1: 1}
        got = run(
            functools.partial(choose_kernel, 1.0 / dp, place, dp == 8),
            ins,
            outs,
            scratch,
            f"choose_{k}",
            in_specs=specs,
            out_specs=out_specs,
            aliases=aliases,
        )
        if not last:
            state["weight_grad"] = got[1]
        state["own", k] = got[0]
        state["sum", k] = lax.ppermute(got[0], "dp", cores)

    def weight_out(name, halves, with_bias=False, last=False):
        ins = [state["own" if own else "sum", k] for k, own in halves]
        halves = [(k, own, near[k]) for k, own in halves]
        n = len(ins)
        extra = [state["own", k] for k in range(3)] if with_bias else []
        outs = [weight_shape] + ([shape((3, outputs), F32)] if with_bias else [])

        scratch = [vm((n, 9, half, outputs), F32), pltpu.SemaphoreType.DMA((n, 7))]
        if with_bias:
            scratch += [vm((3, outputs), F32), pltpu.SemaphoreType.DMA]

        def kernel(*refs):
            main = functools.partial(weight_out_kernel, 1.0 / dp, halves, *refs[:n])
            if with_bias:
                out, bias_out, bufs, sems, buf, sem = refs[-6:]
                copy = bias_kernel(1.0 / dp, body, refs[n : n + 3], bias_out, buf, sem)
                main(out, bufs, sems)
                copy.wait()
            else:
                main(*refs[-3:])

        got = run(
            kernel,
            ins + extra + [state["weight_grad"]],
            outs,
            scratch,
            name,
            in_specs=[whole] * (n + len(extra)) + [anywhere],
            out_specs=[anywhere] * len(outs),
            aliases={n + len(extra): 0},
            last=last,
        )
        state["weight_grad"] = got[0]
        return got[-1]

    def input_part():
        state["back"] = run(
            functools.partial(input_kernel, (columns, stride), parts),
            [weights] + [state["stack", k] for k in range(3)],
            [shape((total, channels), F32)],
            [vm(weights.shape, BF), pltpu.SemaphoreType.DMA],
            "input_grad",
            in_specs=[far] + [whole] * 3,
        )

    two_levels = False

    def send_back():
        counts = [1, 1, 2] if two_levels else [1] * parts
        outs = [shape((n * size, channels), BF) for n in counts]
        back = run(functools.partial(split_rows_kernel, parts), state["back"], outs, [], "split_rows")
        if two_levels:
            state["back"] = [back[0], back[1], exchange(back[2], 0, parts, dp)]
        else:
            state["back"] = [back[0]] + [swap(back[b], b) for b in range(1, parts)]

    def pass_back():
        own, second, got = state["back"]
        outs = [shape((2 * size, channels), BF)]
        on = run(pass_on_kernel, [second, got], outs, [], "pass_on")[0]
        state["back"] = [own, got, exchange(on, 1, parts, dp)]

    def join_back():
        state["input_grad"] = run(
            functools.partial(join_kernel, (rows, columns, stride), parts),
            state["back"],
            [shape(features.shape, BF)],
            [vm((size, channels_all), F32)],
            "join_channels",
        )[0]

    def merge():
        acts = [state["act", k] for k in range(3)]
        state["active"] = run(
            merge_kernel, acts, [shape(grad_out.shape, BF)], [], "merge_branches"
        )[0]

    k0, k1, k2 = 1, 0, 2
    run(touch_kernel, [weights], [], [], "touch_weights", in_specs=[far])
    if top == 2:
        forward(k0, with_feat=True)
        forward(k1)
        reduce_step(k0, 1)
        forward(k2)
        reduce_step(k1, 1)
        activate(k0)
        reduce_step(k2, 1)
        activate(k1)
        gather_step(k0, 0)
        activate(k2)
        gather_step(k1, 0)
        weight_part(k0)
        gather_step(k2, 0)
        add_cores(k0)
        weight_part(k1)
        weight_part(k2)
        add_cores(k1)
        add_cores(k2)
        add_near(k0)
        input_part()
        send_back()
        add_near(k1)
        add_far(k0)
        add_near(k2)
        add_far(k1)
        choose(k0)
        add_far(k2)
        merge()
        join_back()
        choose(k1)
        choose(k2, last=True)
        weight_out("weight_out_a", [(k0, False), (k1, False)])
        bias_grad = weight_out("weight_out_b", [(k2, True)], with_bias=True)
        weight_out("weight_out_c", [(k2, False)], last=True)
    else:
        forward(k0, with_feat=True)
        forward(k1)
        forward(k2)
        for k in (k0, k1, k2):
            for level in range(1, top):
                reduce_step(k, level)
            activate(k)
            for level in range(top - 2, -1, -1):
                gather_step(k, level)
            weight_part(k)
            add_cores(k)
            add_near(k)
        input_part()
        send_back()
        add_far(k0)
        add_far(k1)
        choose(k0)
        add_far(k2)
        join_back()
        merge()
        choose(k1)
        choose(k2, last=True)
        weight_out("weight_out_a", [(k0, False), (k1, False)])
        bias_grad = weight_out("weight_out_b", [(k2, True)], with_bias=True)
        weight_out("weight_out_c", [(k2, False)], last=True)
    return state["active"], state["input_grad"], state["weight_grad"], bias_grad


def solution(mesh):
    placed = (
        P("dp", "space", None, None),
        P(None, None, "space", None),
        P(),
        P("dp", "space", None, None),
    )
    return jax.shard_map(
        per_device,
        mesh=mesh,
        in_specs=placed,
        out_specs=(
            P("dp", "space", None, None),
            P("dp", "space", None, None),
            P(None, None, "space", None),
            P(),
        ),
        check_vma=False,
    )
```
